128 devices in a mesh: seq: 8 (over x_lo, z), res: 16 (over x_hi, y, core).
Axes of the slice: x: 4 (x_hi: 2, x_lo: 2; x = x_hi * 2 + x_lo), y: 4, z: 4, core: 2. Of those that a mesh axis runs over, the one named last changes fastest.
Arguments:
- alignment_features: bfloat16 [96, 1024, 256], P('seq', 'res'), may hold values from -6 to 6
- couple_features: bfloat16 [1024, 1024, 128], P('res', 'seq'), may hold values from -8 to 8
- result_adjoint: bfloat16 [96, 1024, 256], P('seq', 'res'), may hold values from -6 to 6
- asking_projector: bfloat16 [256, 256], replicated, may hold values from -0.375 to 0.375
- lookup_projector: bfloat16 [256, 256], replicated, may hold values from -0.375 to 0.375
- content_projector: bfloat16 [256, 256], replicated, may hold values from -0.375 to 0.375
- sigmoid_projector: bfloat16 [256, 256], replicated, may hold values from -0.375 to 0.375
- final_projector: bfloat16 [256, 256], replicated, may hold values from -0.375 to 0.375
- couple_offset_projector: float32 [128, 8], replicated, may hold values from -8 to 8
- position_real_indicator: int32 [1024], replicated, may hold values from 0 to 1, as said below
- aligned_real_indicator: int32 [96], P('seq'), may hold values 0 or 1
Outputs:
- alignment_derivative: bfloat16 [96, 1024, 256], P('seq', 'res')
- couple_derivative: float32 [1024, 1024, 128], P('res', 'seq')
The draws below stay inside these ranges and needn't reach their ends.
Inputs may be any that keep to these rules, and one draw needn't show every extreme that they name: `position_real_indicator`: the real residues are a leading run of at least 513 residues; the rest is padding.
All inputs are finite; a program needn't handle non-finite values. No bound on the sum of `aligned_real_indicator` on one device may be relied on, other than what follows from the above.
Results may differ from the reference program's by a relative error of at most 0.018.
Values may be sent and summed in bfloat16 or wider, within the bound.
A program may use at most 192 MiB of HBM per device.

```python
import jax
import jax.numpy as jnp
from jax import lax

FEATURE_DEPTH = 256
CZ = 128
HEAD_NUMBER = 8
HEAD_DIM = 32
HIDDEN_SPAN = 256
RES_DEV = 64
ALIGNED_TOTAL = 96
POSITION_TOTAL = 1024


def shared_base(key):
    return jnp.clip(jax.random.normal(key, (CZ, HEAD_NUMBER), jnp.float32), -4.0, 4.0)


def draw_couple_offset_projector(key, part):
    base_table = shared_base(key)
    return base_table * CZ ** (-0.5)


def draw_couple_features(key, part):
    key = jax.random.fold_in(key, 7)
    noise_key = jax.random.fold_in(key, 0)
    noise = jnp.clip(jax.random.normal(noise_key, (POSITION_TOTAL, POSITION_TOTAL, CZ), jnp.float32), -6.0, 6.0)
    return noise.astype(jnp.bfloat16)


def draw_position_real_indicator(key, part):
    key = jax.random.fold_in(key, 3)
    length = jax.random.randint(key, (), POSITION_TOTAL // 2 + 1, POSITION_TOTAL + 1)
    return (jnp.arange(POSITION_TOTAL) < length).astype(jnp.int32)


def with_ends(array, rng, least, largest):
    index_at = [jax.random.randint(jax.random.fold_in(rng, axis), (), 0, length) for axis, length in enumerate(array.shape)]
    longest = array.shape.index(max(array.shape))
    next_to = index_at[:longest] + [(index_at[longest] + 1) % array.shape[longest]] + index_at[longest + 1:]
    return array.at[tuple(index_at)].set(least).at[tuple(next_to)].set(largest)


def steps_of(own_key, dims, cuts, low, high):
    factor_of, own = 1.0, jax.random.fold_in(own_key, 6)
    for dim, parts in cuts:
        heights = jnp.exp(jax.random.uniform(jax.random.fold_in(own, dim), (parts,), jnp.float32, low / len(cuts), high / len(cuts)))
        factor_of = factor_of * jnp.repeat(heights, dims[dim] // parts).reshape([-1 if axis == dim else 1 for axis in range(len(dims))])
    return factor_of


def centred(rng, extent, spread, most, shards=(), kind=jnp.bfloat16):
    values = jax.random.normal(rng, extent, jnp.float32) * spread
    if len(shards) > 0:
        values = steps_of(rng, extent, shards, -0.22, 0.18) * values
    return jnp.clip(values, min=-most, max=most).astype(kind)


def setup_inputs(seed: int = 0) -> dict:
    arg_keys = jax.random.split(jax.random.key(seed), 12)
    alignment_features = centred(arg_keys[0], (ALIGNED_TOTAL, POSITION_TOTAL, FEATURE_DEPTH), 1.0, 6.0, ((0, 8), (1, 16)))
    couple_features = draw_couple_features(jax.random.fold_in(arg_keys[11], 71), 0)
    result_adjoint = centred(arg_keys[2], (ALIGNED_TOTAL, POSITION_TOTAL, FEATURE_DEPTH), 1.0, 6.0, ((0, 8), (1, 16)))
    asking_projector = centred(arg_keys[3], (FEATURE_DEPTH, HIDDEN_SPAN), FEATURE_DEPTH ** -0.5, 0.375)
    lookup_projector = centred(arg_keys[4], (FEATURE_DEPTH, HIDDEN_SPAN), FEATURE_DEPTH ** -0.5, 0.375)
    content_projector = centred(arg_keys[5], (FEATURE_DEPTH, HIDDEN_SPAN), FEATURE_DEPTH ** -0.5, 0.375)
    sigmoid_projector = centred(arg_keys[6], (FEATURE_DEPTH, HIDDEN_SPAN), FEATURE_DEPTH ** -0.5, 0.375)
    final_projector = centred(arg_keys[7], (HIDDEN_SPAN, FEATURE_DEPTH), HIDDEN_SPAN ** -0.5, 0.375)
    couple_offset_projector = draw_couple_offset_projector(jax.random.fold_in(arg_keys[11], 71), 0)
    position_real_indicator = draw_position_real_indicator(jax.random.fold_in(arg_keys[11], 71), 0)
    aligned_real_indicator = with_ends((jax.random.randint(arg_keys[10], (ALIGNED_TOTAL,), 0, 4) < 3).astype(jnp.int32), jax.random.fold_in(arg_keys[10], 1), 0, 1)
    return {"alignment_features": alignment_features, "couple_features": couple_features, "result_adjoint": result_adjoint, "asking_projector": asking_projector, "lookup_projector": lookup_projector, "content_projector": content_projector, "sigmoid_projector": sigmoid_projector, "final_projector": final_projector, "couple_offset_projector": couple_offset_projector, "position_real_indicator": position_real_indicator, "aligned_real_indicator": aligned_real_indicator}


def centering_module(values_in):
    row_mean = lax.optimization_barrier(jnp.mean(values_in, -1, keepdims=True))
    centered = values_in - row_mean
    variance = lax.optimization_barrier(jnp.mean(centered * centered, -1, keepdims=True))
    return centered * lax.rsqrt(variance + 1e-05)

def tile_bias(pair_tile, couple_offset_projector):
    return jnp.einsum('ijc,ch->hij', centering_module(pair_tile), couple_offset_projector, precision=lax.Precision.HIGHEST)

def reference(alignment_features, couple_features, result_adjoint, asking_projector, lookup_projector, content_projector, sigmoid_projector, final_projector, couple_offset_projector, position_real_indicator, aligned_real_indicator):
    score_scale = HEAD_DIM ** (-0.5)
    blocks = couple_features.reshape(POSITION_TOTAL // RES_DEV, RES_DEV, POSITION_TOTAL, CZ)
    bias_blocks = lax.map(lambda blk: tile_bias(blk.astype(jnp.float32), couple_offset_projector), blocks)
    pair_bias = bias_blocks.transpose(1, 0, 2, 3).reshape(HEAD_NUMBER, POSITION_TOTAL, POSITION_TOTAL)
    usable = position_real_indicator > 0

    def alone_aligned_entry(offset_derivative, bundled_operands):
        alone_alignment_line, line_derivative, line_retain_indicator = bundled_operands
        alignment_real = alone_alignment_line.astype(jnp.float32)
        standardized_couple = centering_module(alignment_real).astype(jnp.bfloat16)
        queries = (jnp.dot(standardized_couple, asking_projector, preferred_element_type=jnp.float32) * score_scale).astype(jnp.bfloat16)
        keys_all = jnp.dot(standardized_couple, lookup_projector, preferred_element_type=jnp.float32).astype(jnp.bfloat16)
        values_all = jnp.dot(standardized_couple, content_projector, preferred_element_type=jnp.float32).astype(jnp.bfloat16)
        gate_act = jax.nn.sigmoid(jnp.dot(standardized_couple, sigmoid_projector, preferred_element_type=jnp.float32))
        q_heads = queries.reshape(POSITION_TOTAL, HEAD_NUMBER, HEAD_DIM).astype(jnp.float32)
        k_heads = keys_all.reshape(POSITION_TOTAL, HEAD_NUMBER, HEAD_DIM).astype(jnp.float32)
        v_heads = values_all.reshape(POSITION_TOTAL, HEAD_NUMBER, HEAD_DIM).astype(jnp.float32)
        logits = jnp.einsum('ihd,jhd->hij', q_heads, k_heads) + pair_bias
        logits = jnp.where(usable[None, None, :], logits, -1000000000.0)
        attn_probs = jax.nn.softmax(logits, axis=-1)
        prob_half = attn_probs.astype(jnp.bfloat16)
        attended = jnp.einsum('hij,jhd->ihd', prob_half.astype(jnp.float32), v_heads).reshape(POSITION_TOTAL, HIDDEN_SPAN)
        grad_in = line_derivative * line_retain_indicator.astype(jnp.bfloat16)
        d_gated = jnp.dot(grad_in, final_projector.T, preferred_element_type=jnp.float32)
        d_attended = (d_gated * gate_act).astype(jnp.bfloat16).reshape(POSITION_TOTAL, HEAD_NUMBER, HEAD_DIM).astype(jnp.float32)
        d_gate = (d_gated * attended * gate_act * (1.0 - gate_act)).astype(jnp.bfloat16)
        d_probs = jnp.einsum('ihd,jhd->hij', d_attended, v_heads)
        d_values = jnp.einsum('hij,ihd->jhd', prob_half.astype(jnp.float32), d_attended).reshape(POSITION_TOTAL, HIDDEN_SPAN)
        d_logits = attn_probs * (d_probs - lax.optimization_barrier(jnp.sum(attn_probs * d_probs, -1, keepdims=True)))
        dlog_half = d_logits.astype(jnp.bfloat16).astype(jnp.float32)
        d_queries = (score_scale * jnp.einsum('hij,jhd->ihd', dlog_half, k_heads)).astype(jnp.bfloat16).reshape(POSITION_TOTAL, HIDDEN_SPAN)
        d_keys = jnp.einsum('hij,ihd->jhd', dlog_half, q_heads).reshape(POSITION_TOTAL, HIDDEN_SPAN)
        standardized_derivative = jnp.dot(d_queries, asking_projector.T, preferred_element_type=jnp.float32)
        standardized_derivative = standardized_derivative + jnp.dot(d_gate, sigmoid_projector.T, preferred_element_type=jnp.float32)
        standardized_derivative = standardized_derivative + jnp.dot(d_keys, lookup_projector.astype(jnp.float32).T, precision=lax.Precision.HIGHEST)
        standardized_derivative = standardized_derivative + jnp.dot(d_values, content_projector.astype(jnp.float32).T, precision=lax.Precision.HIGHEST)
        discarded_result, adjoint_mapping = jax.vjp(centering_module, alignment_real)
        d_row = adjoint_mapping(standardized_derivative)[0].astype(jnp.bfloat16)
        return (offset_derivative + d_logits, d_row)
    offset_derivative, alignment_derivative = lax.scan(alone_aligned_entry, jnp.zeros((HEAD_NUMBER, POSITION_TOTAL, POSITION_TOTAL), jnp.float32), (alignment_features, result_adjoint, aligned_real_indicator))
    cot_blocks = offset_derivative.reshape(HEAD_NUMBER, POSITION_TOTAL // RES_DEV, RES_DEV, POSITION_TOTAL).transpose(1, 0, 2, 3)

    def pair_grad(bundled_operands):
        pair_tile, cot_tile = bundled_operands
        discarded_result, adjoint_mapping = jax.vjp(lambda tile_in: tile_bias(tile_in, couple_offset_projector), pair_tile.astype(jnp.float32))
        return adjoint_mapping(cot_tile)[0]
    couple_derivative = lax.map(pair_grad, (blocks, cot_blocks)).reshape(POSITION_TOTAL, POSITION_TOTAL, CZ)
    return (alignment_derivative, couple_derivative)
```

```python
import jax
import jax.numpy as jnp
from jax import lax
from jax.experimental import pallas as pl
from jax.experimental.pallas import tpu as pltpu
from jax.sharding import PartitionSpec as P

BF = jnp.bfloat16
F32 = jnp.float32
MESH = pl.DeviceIdType.MESH
EPS = 1e-05

SEQS = 6
ROWS = 128
HALF = 64
RES = 1024
WIDTH = 256
HEADS = 8
HD = 32
PEERS = 8
CH = 2
NCH = HEADS // CH

NN = (((1,), (0,)), ((), ()))
NT = (((1,), (1,)), ((), ()))
TT = (((0,), (1,)), ((), ()))


def dot(a, b, dims=NN):
    return lax.dot_general(a, b, dims, preferred_element_type=F32)


def layer_norm_parts(x):
    mean = jnp.mean(x, -1, keepdims=True)
    cen = x - mean
    var = jnp.mean(cen * cen, -1, keepdims=True)
    rstd = lax.rsqrt(var + EPS)
    return cen * rstd, rstd


def split(x):
    hi = x.astype(BF)
    return hi, (x - hi.astype(F32)).astype(BF)


def main_kernel(
    x_ref, pair_ref, g_ref, wq, wk, wv, wg, wo, wp_ref, mask_ref, keep_ref,
    out_ref, dtile_ref,
    xraw, graw, xg, bias, dbias, btmp, kt, vt, q_s, do_s, doT, qT, o_s, dq_s, dkt, dvt,
    dnear, dfar, rsbuf, ostage, orecv, dxs, dxr, dbs, dbr,
    sx_s, sx_r, ag_s, ag_r, rs_s, rs_r, bi_s, bi_r, bf_s, bf_r, dx_s, dx_r, ds_s, ds_r, oo_s, oo_r,
):
    sq = lax.axis_index("seq")
    rs = lax.axis_index("res")
    p = lax.rem(rs, 2)
    c = lax.div(rs, 2)
    other = 1 - p
    partner = (sq, rs + 1 - 2 * p)

    def res_peer(d):
        return (sq, lax.rem(c + d, PEERS) * 2 + p)

    def seq_peer(d):
        return (lax.rem(sq + d, PEERS), rs)

    bar = pltpu.get_barrier_semaphore()
    pl.semaphore_signal(bar, inc=1, device_id=partner, device_id_type=MESH)
    for d in range(1, PEERS):
        pl.semaphore_signal(bar, inc=1, device_id=res_peer(d), device_id_type=MESH)
        pl.semaphore_signal(bar, inc=1, device_id=seq_peer(d), device_id_type=MESH)
    pl.semaphore_wait(bar, 2 * PEERS - 1)

    my_rows = pl.ds(pl.multiple_of(p * HALF, HALF), HALF)
    other_rows = pl.ds(pl.multiple_of(other * HALF, HALF), HALF)
    chip_rows = pl.ds(pl.multiple_of(c * ROWS, ROWS), ROWS)
    my_cols = pl.ds(pl.multiple_of(sq * ROWS, ROWS), ROWS)

    def swap_copy(i, src, dst):
        return pltpu.make_async_remote_copy(
            src.at[pl.ds(other * SEQS, SEQS)], dst.at[:, my_rows, :], sx_s.at[i], sx_r.at[i],
            device_id=partner, device_id_type=MESH,
        )

    swaps = [swap_copy(0, x_ref, xraw), swap_copy(1, g_ref, graw)]
    for cp in swaps:
        cp.start()
    xraw[:, my_rows, :] = x_ref[pl.ds(p * SEQS, SEQS)]
    graw[:, my_rows, :] = g_ref[pl.ds(p * SEQS, SEQS)]

    def gather_copy(s, d):
        blk = xg.at[s, chip_rows, :]
        return pltpu.make_async_remote_copy(
            blk, blk, ag_s.at[s, d], ag_r.at[s, d], device_id=res_peer(d), device_id_type=MESH
        )

    for cp in swaps:
        cp.wait_recv()

    def norm_body(s, carry):
        xhat, rstd = layer_norm_parts(xraw[s].astype(F32))
        xg[s, chip_rows, :] = xhat.astype(BF)
        for d in range(1, PEERS):
            gather_copy(s, d).start()
        return carry

    lax.fori_loop(0, SEQS, norm_body, 0)

    w_hi, w_lo = split(wp_ref[...].T)
    left = jnp.concatenate(
        [jnp.concatenate([w_hi, w_hi], 1), jnp.concatenate([w_lo, jnp.zeros_like(w_lo)], 1)], 0
    )
    ones = jnp.ones((8, WIDTH), BF)

    def pair_body(i, carry):
        x = pair_ref[i].astype(F32)
        cen = x - jnp.mean(x, -1, keepdims=True)
        c_hi, c_lo = split(cen)
        s_hi, s_lo = split(cen * cen)
        y = dot(left, jnp.concatenate([c_hi, c_lo], 1), NT)
        var = dot(ones, jnp.concatenate([s_hi, s_lo], 1), NT) * (1.0 / 128)
        btmp[pl.ds(pl.multiple_of(i * 8, 8), 8), :] = (y[0:8] + y[8:16]) * lax.rsqrt(var + EPS)
        return carry

    lax.fori_loop(0, HALF, pair_body, 0, unroll=8)

    def bias_copy(k, d):
        blk = bias.at[pl.ds(k * CH, CH), my_rows, my_cols]
        return pltpu.make_async_remote_copy(
            blk, blk, bi_s.at[k, d], bi_r.at[k, d], device_id=seq_peer(d), device_id_type=MESH
        )

    def forward_copy(k):
        blk = bias.at[pl.ds(k * CH, CH), my_rows, :]
        return pltpu.make_async_remote_copy(
            blk, blk, bf_s.at[k], bf_r.at[k], device_id=partner, device_id_type=MESH
        )

    usable = mask_ref[pl.ds(sq, 1), :] > 0
    for k in range(NCH):
        for h in range(k * CH, k * CH + CH):
            bias[h, my_rows, my_cols] = jnp.where(
                usable, btmp[pl.ds(h, HALF, stride=8), :], -1000000000.0
            )
        for d in range(1, PEERS):
            bias_copy(k, d).start()

    def bias_arrive(k):
        for d in range(1, PEERS):
            bias_copy(k, d).wait_recv()
        forward_copy(k).start()

    def scatter_copy(s, d):
        cols = pl.ds(pl.multiple_of(lax.rem(c + d, PEERS) * ROWS, ROWS), ROWS)
        return pltpu.make_async_remote_copy(
            dfar.at[s, :, cols], rsbuf.at[s, d], rs_s.at[s, d], rs_r.at[s, d],
            device_id=res_peer(d), device_id_type=MESH,
        )

    dbias[...] = jnp.zeros_like(dbias)
    scale = HD ** (-0.5)

    def finish_seq(s):
        for d in range(1, PEERS):
            scatter_copy(s, d).wait_recv()
        far = dfar[s, :, chip_rows].astype(F32)
        for d in range(1, PEERS):
            far = far + rsbuf[s, d].astype(F32)
        dn = dnear[s] + far.T
        xhat, rstd = layer_norm_parts(xraw[s].astype(F32))
        dx = rstd * (
            dn
            - jnp.mean(dn, -1, keepdims=True)
            - xhat * jnp.mean(dn * xhat, -1, keepdims=True)
        )
        ostage[s] = dx.astype(BF)

    def seq_body(s, carry):
        for d in range(1, PEERS):
            gather_copy(s, d).wait_recv()
        x = xg[s]
        kt[...] = dot(wk[...], x, TT).astype(BF)
        vt[...] = dot(wv[...], x, TT).astype(BF)
        xq = xg[s, chip_rows, :]
        qf = dot(xq, wq[...]) * scale
        q_s[...] = qf.astype(BF)
        qT[...] = qf.T.astype(BF)
        gate = jax.nn.sigmoid(dot(xq, wg[...]))
        keep = keep_ref[p * SEQS + s].astype(F32)
        grad_in = (graw[s].astype(F32) * keep).astype(BF)
        dg = dot(grad_in, wo[...], NT)
        d_att = dg * gate
        do_s[...] = d_att.astype(BF)
        doT[...] = d_att.T.astype(BF)

        @pl.when(s == 0)
        def _():
            bias_arrive(0)

        for h in range(HEADS):
            hs = slice(HD * h, HD * h + HD)
            if h % CH == 0:
                k = h // CH

                @pl.when(s == 0)
                def _():
                    if k + 1 < NCH:
                        bias_arrive(k + 1)
                    forward_copy(k).wait_recv()

            logits = dot(q_s[:, hs], kt[hs, :]) + bias[h]
            top = jnp.max(logits, -1, keepdims=True)
            e = jnp.exp(logits - top)
            prob = e * (1.0 / jnp.sum(e, -1, keepdims=True))
            prob_half = prob.astype(BF)
            d_prob = dot(do_s[:, hs], vt[hs, :])
            att = dot(prob_half, vt[hs, :], NT)
            o_s[:, hs] = att
            inner = jnp.sum(att * do_s[:, hs].astype(F32), -1, keepdims=True)
            d_log = prob * (d_prob - inner)
            dbias[h] += d_log
            dlog_half = d_log.astype(BF)
            dq_s[:, hs] = (dot(dlog_half, kt[hs, :], NT) * scale).astype(BF)
            dvt[hs, :] = dot(doT[hs, :], prob_half).astype(BF)
            dkt[hs, :] = dot(qT[hs, :], dlog_half).astype(BF)

        d_gate = (dg * o_s[...] * gate * (1.0 - gate)).astype(BF)
        dnear[s] = dot(dq_s[...], wq[...], NT) + dot(d_gate, wg[...], NT)
        dfar[s] = (dot(wk[...], dkt[...]) + dot(wv[...], dvt[...])).astype(BF)
        for d in range(1, PEERS):
            scatter_copy(s, d).start()

        @pl.when(s >= 2)
        def _():
            finish_seq(s - 2)

        return carry

    lax.fori_loop(0, SEQS, seq_body, 0)

    def pair_swap(k):
        blk = pl.ds(k * CH, CH)
        return pltpu.make_async_remote_copy(
            dxs.at[blk], dxr.at[blk], dx_s.at[k], dx_r.at[k], device_id=partner, device_id_type=MESH
        )

    def tile_copy(k, d):
        cols = pl.ds(pl.multiple_of(lax.rem(sq + d, PEERS) * ROWS, ROWS), ROWS)
        blk = pl.ds(k * CH, CH)
        return pltpu.make_async_remote_copy(
            dbs.at[blk, :, cols], dbr.at[d, blk], ds_s.at[k, d], ds_r.at[k, d],
            device_id=seq_peer(d), device_id_type=MESH,
        )

    for k in range(NCH):
        blk = pl.ds(k * CH, CH)
        dxs[blk] = dbias[blk, other_rows, :].astype(BF)
        pair_swap(k).start()
    for k in range(NCH):
        blk = pl.ds(k * CH, CH)
        pair_swap(k).wait_recv()
        dbs[blk] = (dbias[blk, my_rows, :] + dxr[blk].astype(F32)).astype(BF)
        for d in range(1, PEERS):
            tile_copy(k, d).start()

    finish_seq(SEQS - 2)
    finish_seq(SEQS - 1)
    back = pltpu.make_async_remote_copy(
        ostage.at[:, other_rows, :], orecv, oo_s, oo_r, device_id=partner, device_id_type=MESH
    )
    back.start()
    out_ref[pl.ds(p * SEQS, SEQS)] = ostage[:, my_rows, :]

    for k in range(NCH):
        blk = pl.ds(k * CH, CH)
        for d in range(1, PEERS):
            tile_copy(k, d).wait_recv()
        tile = dbs[blk, :, my_cols].astype(F32)
        for d in range(1, PEERS):
            tile = tile + dbr[d, blk].astype(F32)
        dtile_ref[blk] = tile

    back.wait_recv()
    out_ref[pl.ds(other * SEQS, SEQS)] = orecv[...]

    for cp in swaps:
        cp.wait_send()
    back.wait_send()

    def drain_seq(s, carry):
        for d in range(1, PEERS):
            gather_copy(s, d).wait_send()
            scatter_copy(s, d).wait_send()
        return carry

    lax.fori_loop(0, SEQS, drain_seq, 0)

    def drain_chunk(k, carry):
        forward_copy(k).wait_send()
        pair_swap(k).wait_send()
        for d in range(1, PEERS):
            bias_copy(k, d).wait_send()
            tile_copy(k, d).wait_send()
        return carry

    lax.fori_loop(0, NCH, drain_chunk, 0)


def run_main(x, pair, g, wq, wk, wv, wg, wo, wp, mask, keep):
    def vm(*shape, dt=BF):
        return pltpu.VMEM(shape, dt)

    dma = pltpu.SemaphoreType.DMA
    vmem = pl.BlockSpec(memory_space=pltpu.VMEM)
    smem = pl.BlockSpec(memory_space=pltpu.SMEM)
    return pl.pallas_call(
        main_kernel,
        out_shape=(
            jax.ShapeDtypeStruct(x.shape, BF),
            jax.ShapeDtypeStruct((HEADS, HALF, ROWS), F32),
        ),
        in_specs=[vmem] * 10 + [smem],
        out_specs=[vmem, vmem],
        scratch_shapes=[
            vm(SEQS, ROWS, WIDTH),
            vm(SEQS, ROWS, WIDTH),
            vm(SEQS, RES, WIDTH),
            vm(HEADS, ROWS, RES, dt=F32),
            vm(HEADS, ROWS, RES, dt=F32),
            vm(HALF * 8, ROWS, dt=F32),
            vm(WIDTH, RES),
            vm(WIDTH, RES),
            vm(ROWS, WIDTH),
            vm(ROWS, WIDTH),
            vm(WIDTH, ROWS),
            vm(WIDTH, ROWS),
            vm(ROWS, WIDTH, dt=F32),
            vm(ROWS, WIDTH),
            vm(WIDTH, RES),
            vm(WIDTH, RES),
            vm(SEQS, ROWS, WIDTH, dt=F32),
            vm(SEQS, WIDTH, RES),
            vm(SEQS, PEERS, WIDTH, ROWS),
            vm(SEQS, ROWS, WIDTH),
            vm(SEQS, HALF, WIDTH),
            vm(HEADS, HALF, RES),
            vm(HEADS, HALF, RES),
            vm(HEADS, HALF, RES),
            vm(PEERS, HEADS, HALF, ROWS),
            dma((2,)), dma((2,)),
            dma((SEQS, PEERS)), dma((SEQS, PEERS)),
            dma((SEQS, PEERS)), dma((SEQS, PEERS)),
            dma((NCH, PEERS)), dma((NCH, PEERS)),
            dma((NCH,)), dma((NCH,)),
            dma((NCH,)), dma((NCH,)),
            dma((NCH, PEERS)), dma((NCH, PEERS)),
            dma, dma,
        ],
        compiler_params=pltpu.CompilerParams(
            collective_id=0, has_side_effects=True, vmem_limit_bytes=56 * 2**20
        ),
        name="attention_backward",
    )(x, pair, g, wq, wk, wv, wg, wo, wp, mask, keep)


PB = 8


def pair_kernel(pair_ref, d_ref, wp_ref, out_ref):
    w_hi, w_lo = split(wp_ref[...].T)
    w2 = jnp.concatenate([w_hi, w_lo, w_hi, w_lo], 0)
    for i in range(PB):
        xhat, rstd = layer_norm_parts(pair_ref[i].astype(F32))
        d_hi, d_lo = split(d_ref[:, i, :])
        dn = lax.dot_general(
            jnp.concatenate([d_hi, d_hi, d_lo, d_lo], 0), w2, (((0,), (0,)), ((), ())),
            preferred_element_type=F32,
        )
        out_ref[i] = rstd * (
            dn
            - jnp.mean(dn, -1, keepdims=True)
            - xhat * jnp.mean(dn * xhat, -1, keepdims=True)
        )


def run_pair(pair, dtile, wp):
    n = pair.shape[0]
    return pl.pallas_call(
        pair_kernel,
        grid=(n // PB,),
        out_shape=jax.ShapeDtypeStruct(pair.shape, F32),
        in_specs=[
            pl.BlockSpec((PB, 128, 128), lambda i: (i, 0, 0)),
            pl.BlockSpec((HEADS, PB, 128), lambda i: (0, i, 0)),
            pl.BlockSpec((128, HEADS), lambda i: (0, 0)),
        ],
        out_specs=pl.BlockSpec((PB, 128, 128), lambda i: (i, 0, 0)),
        name="pair_gradient",
    )(pair, dtile, wp)


def body(x, pair, g, wq, wk, wv, wg, wo, wp, mask, keep):
    dx, dtile = run_main(x, pair, g, wq, wk, wv, wg, wo, wp, mask.reshape(8, 128), keep)
    return dx, run_pair(pair, dtile, wp)


def solution(mesh):
    return jax.shard_map(
        body,
        mesh=mesh,
        in_specs=(
            P("seq", "res", None),
            P("res", "seq", None),
            P("seq", "res", None),
            P(),
            P(),
            P(),
            P(),
            P(),
            P(),
            P(),
            P("seq"),
        ),
        out_specs=(P("seq", "res", None), P("res", "seq", None)),
        check_vma=False,
    )
```

```python
import jax
import jax.numpy as jnp
from jax import lax
from jax.experimental import pallas as pl
from jax.experimental.pallas import tpu as pltpu
from jax.sharding import PartitionSpec as P

BF = jnp.bfloat16
F32 = jnp.float32
MESH = pl.DeviceIdType.MESH
EPS = 1e-05

SEQS = 6
ROWS = 128
HALF = 64
RES = 1024
WIDTH = 256
HEADS = 8
HD = 32
PEERS = 8
CH = 2
NCH = HEADS // CH
COEF = 16

NN = (((1,), (0,)), ((), ()))
NT = (((1,), (1,)), ((), ()))
TT = (((0,), (1,)), ((), ()))


def dot(a, b, dims=NN):
    return lax.dot_general(a, b, dims, preferred_element_type=F32)


def layer_norm_parts(x):
    mean = jnp.mean(x, -1, keepdims=True)
    cen = x - mean
    var = jnp.mean(cen * cen, -1, keepdims=True)
    rstd = lax.rsqrt(var + EPS)
    return cen * rstd, rstd


def split(x):
    hi = x.astype(BF)
    return hi, (x - hi.astype(F32)).astype(BF)


def main_kernel(
    x_ref, pair_ref, g_ref, wq, wk, wv, wg, wo, wpt_ref, mask_ref, keep_ref,
    out_ref, coef_ref,
    xraw, graw, xg, bias, dbias, btmp, stat, kt, vt, q_s, do_s, doT, qT, o_s, dq_s, dkt, dvt,
    dg_s, gt_s, dnear, dfar, rsbuf, ostage, orecv, dxs, dxr, dbs, dbr,
    sx_s, sx_r, ag_s, ag_r, rs_s, rs_r, bi_s, bi_r, bf_s, bf_r, dx_s, dx_r, ds_s, ds_r, oo_s, oo_r,
):
    sq = lax.axis_index("seq")
    rs = lax.axis_index("res")
    p = lax.rem(rs, 2)
    other = 1 - p
    y = lax.rem(lax.div(rs, 2), 4)
    xhi = lax.div(rs, 8)
    z = lax.rem(sq, 4)
    xlo = lax.div(sq, 4)
    partner = (sq, rs + 1 - 2 * p)
    x_peer = (sq, (1 - xhi) * 8 + y * 2 + p)
    lo_peer = ((1 - xlo) * 4 + z, rs)

    def ring(at, step):
        return lax.rem(at + step, 4)

    def y_peer(e):
        return (sq, xhi * 8 + ring(y, e) * 2 + p)

    def z_peer(e):
        return (xlo * 4 + ring(z, e), rs)

    def res_peer(i):
        hi = xhi if i < 4 else 1 - xhi
        return (sq, hi * 8 + ring(y, i % 4) * 2 + p)

    def seq_peer(i):
        hi = xlo if i < 4 else 1 - xlo
        return (hi * 4 + ring(z, i % 4), rs)

    def block(hi, at):
        return pl.ds(pl.multiple_of((hi * 4 + at) * ROWS, ROWS), ROWS)

    bar = pltpu.get_barrier_semaphore()
    for dev in [partner] + [f(i) for i in range(1, PEERS) for f in (res_peer, seq_peer)]:
        pl.semaphore_signal(bar, inc=1, device_id=dev, device_id_type=MESH)

    my_rows = pl.ds(pl.multiple_of(p * HALF, HALF), HALF)
    other_rows = pl.ds(pl.multiple_of(other * HALF, HALF), HALF)
    chip_rows = block(xhi, y)
    my_cols = block(xlo, z)

    def send(src, dst, s_sem, r_sem, dev):
        return pltpu.make_async_remote_copy(
            src_ref=src, dst_ref=dst, send_sem=s_sem, recv_sem=r_sem,
            device_id=dev, device_id_type=MESH,
        )

    def swap_copy(i, src, dst):
        return send(
            src.at[pl.ds(other * SEQS, SEQS)], dst.at[:, my_rows, :], sx_s.at[i], sx_r.at[i], partner
        )

    def gather_copy(s, e):
        blk = xg.at[s, chip_rows, :]
        return send(blk, blk, ag_s.at[s, e], ag_r.at[s, e], x_peer if e == 4 else y_peer(e))

    def gather_on(s, e, along_y):
        if along_y:
            blk, dev = xg.at[s, block(1 - xhi, y), :], y_peer(e)
        else:
            blk, dev = xg.at[s, block(xhi, ring(y, 4 - e)), :], x_peer
        return send(blk, blk, ag_s.at[s, 4 + e], ag_r.at[s, 4 + e], dev)

    def gather_first(s):
        for e in (4, 1, 2, 3):
            gather_copy(s, e).start()

    def gather_second(s):
        @pl.when(lax.rem(s, 2) == 0)
        def _():
            gather_copy(s, 4).wait_recv()
            for e in (1, 2, 3):
                gather_on(s, e, True).start()

        @pl.when(lax.rem(s, 2) == 1)
        def _():
            for e in (1, 2, 3):
                gather_copy(s, e).wait_recv()
                gather_on(s, e, False).start()

    def gather_rest(s):
        @pl.when(lax.rem(s, 2) == 0)
        def _():
            for e in (1, 2, 3):
                gather_copy(s, e).wait_recv()

        @pl.when(lax.rem(s, 2) == 1)
        def _():
            gather_copy(s, 4).wait_recv()

        for e in (1, 2, 3):
            gather_on(s, e, True).wait_recv()

    w_hi, w_lo = split(wpt_ref[...])
    left = jnp.concatenate(
        [jnp.concatenate([w_hi, w_hi], 1), jnp.concatenate([w_lo, jnp.zeros_like(w_lo)], 1)], 0
    )
    ones = jnp.ones((8, WIDTH), BF)
    square = jnp.full((128, 128), 1.0 / 128, BF)
    top_row = lax.broadcasted_iota(jnp.int32, (8, 128), 0) == 0

    def pair_body(i, carry):
        xb = pair_ref[i]
        cen = xb.astype(F32) - dot(xb, square)
        c_hi, c_lo = split(cen)
        s_hi, s_lo = split(cen * cen)
        proj = dot(left, jnp.concatenate([c_hi, c_lo], 1), NT)
        var = dot(ones, jnp.concatenate([s_hi, s_lo], 1), NT) * (1.0 / 128)
        mean = dot(ones[:, :128], xb, NT) * (1.0 / 128)
        rstd = lax.rsqrt(var + EPS)
        at = pl.ds(pl.multiple_of(i * 8, 8), 8)
        btmp[at, :] = (proj[0:8] + proj[8:16]) * rstd
        stat[at, :] = jnp.where(top_row, mean, rstd)
        return carry

    lax.fori_loop(0, HALF // 2, pair_body, 0, unroll=8)
    pl.semaphore_wait(bar, 2 * PEERS - 1)
    swaps = [swap_copy(0, x_ref, xraw), swap_copy(1, g_ref, graw)]
    for cp in swaps:
        cp.start()
    xraw[:, my_rows, :] = x_ref[pl.ds(p * SEQS, SEQS)]
    graw[:, my_rows, :] = g_ref[pl.ds(p * SEQS, SEQS)]

    lax.fori_loop(HALF // 2, HALF, pair_body, 0, unroll=8)

    def bias_copy(k, e):
        blk = bias.at[pl.ds(k * CH, CH), my_rows, my_cols]
        return send(blk, blk, bi_s.at[k, e], bi_r.at[k, e], lo_peer if e == 4 else z_peer(e))

    def bias_on(k, e):
        if k % 2 == 0:
            cols, dev = block(1 - xlo, z), z_peer(e)
        else:
            cols, dev = block(xlo, ring(z, 4 - e)), lo_peer
        blk = bias.at[pl.ds(k * CH, CH), my_rows, cols]
        return send(blk, blk, bi_s.at[k, 4 + e], bi_r.at[k, 4 + e], dev)

    def forward_copy(k):
        blk = bias.at[pl.ds(k * CH, CH), my_rows, :]
        return send(blk, blk, bf_s.at[k], bf_r.at[k], partner)

    usable = mask_ref[pl.ds(sq, 1), :] > 0
    for k in range(NCH):
        for h in range(k * CH, k * CH + CH):
            bias[h, my_rows, my_cols] = jnp.where(
                usable, btmp[pl.ds(h, HALF, stride=8), :], -1000000000.0
            )
        bias_copy(k, 4).start()

    def bias_first(k):
        for e in (1, 2, 3):
            bias_copy(k, e).start()

    bias_first(0)
    bias_first(1)

    def bias_second(k):
        if k % 2 == 0:
            bias_copy(k, 4).wait_recv()
            for e in (1, 2, 3):
                bias_on(k, e).start()
        else:
            for e in (1, 2, 3):
                bias_copy(k, e).wait_recv()
                bias_on(k, e).start()

    def bias_arrive(k):
        if k % 2 == 0:
            for e in (1, 2, 3):
                bias_copy(k, e).wait_recv()
        else:
            bias_copy(k, 4).wait_recv()
        for e in (1, 2, 3):
            bias_on(k, e).wait_recv()
        forward_copy(k).start()

    def norm(s):
        xhat, rstd = layer_norm_parts(xraw[s].astype(F32))
        xg[s, chip_rows, :] = xhat.astype(BF)

    def norm_body(s, carry):
        norm(s)
        return carry

    swaps[0].wait_recv()
    for s in (0, 1):
        norm(s)
        gather_first(s)
    lax.fori_loop(2, SEQS, norm_body, 0)
    bias_second(0)
    bias_first(2)
    gather_second(0)
    gather_first(2)
    gather_second(1)
    bias_second(1)
    bias_first(3)
    gather_first(3)
    bias_second(2)
    swaps[1].wait_recv()

    def scatter_y(s, e, hi):
        row = xhi if hi == 0 else 1 - xhi
        i = e + 3 * hi
        return send(
            dfar.at[s, :, block(row, ring(y, e))], rsbuf.at[s, i], rs_s.at[s, i], rs_r.at[s, i], y_peer(e)
        )

    def scatter_x_on(s):
        return send(
            dfar.at[s, :, block(1 - xhi, y)], rsbuf.at[s, 7], rs_s.at[s, 7], rs_r.at[s, 7], x_peer
        )

    def scatter_x(s, e):
        return send(
            dfar.at[s, :, block(1 - xhi, ring(y, e))], rsbuf.at[s, e], rs_s.at[s, e], rs_r.at[s, e], x_peer
        )

    def scatter_y_on(s, e):
        return send(
            dfar.at[s, :, block(xhi, ring(y, e))], rsbuf.at[s, 4 + e], rs_s.at[s, 4 + e], rs_r.at[s, 4 + e],
            y_peer(e),
        )

    def scatter_one(s, i):
        hi = xhi if i < 4 else 1 - xhi
        return send(
            dfar.at[s, :, block(hi, ring(y, i % 4))], rsbuf.at[s, i], rs_s.at[s, i], rs_r.at[s, i], res_peer(i)
        )

    def total(first, parts):
        out = first.astype(F32)
        for part in parts:
            out = out + part.astype(F32)
        return out

    def scatter_first(s):
        @pl.when(lax.rem(s, 2) == 0)
        def _():
            for e in (1, 2, 3):
                scatter_y(s, e, 1).start()
            for e in (1, 2, 3):
                scatter_y(s, e, 0).start()

        @pl.when(lax.rem(s, 2) == 1)
        def _():
            for e in (1, 2, 3, 0):
                scatter_x(s, e).start()

    def scatter_second(s):
        @pl.when(lax.rem(s, 2) == 0)
        def _():
            for e in (1, 2, 3):
                scatter_y(s, e, 1).wait_recv()
            blk = block(1 - xhi, y)
            dfar[s, :, blk] = total(dfar[s, :, blk], [rsbuf[s, 3 + e] for e in (1, 2, 3)]).astype(BF)
            scatter_x_on(s).start()

        @pl.when(lax.rem(s, 2) == 1)
        def _():
            for e in (1, 2, 3):
                scatter_x(s, e).wait_recv()
                blk = block(xhi, ring(y, e))
                dfar[s, :, blk] = total(dfar[s, :, blk], [rsbuf[s, e]]).astype(BF)
                scatter_y_on(s, e).start()

    def scatter_last(s):
        @pl.when(lax.rem(s, 2) == 0)
        def _():
            for e in (1, 2, 3):
                scatter_y(s, e, 0).wait_recv()
            scatter_x_on(s).wait_recv()
            finish_seq(s, total(dfar[s, :, chip_rows], [rsbuf[s, e] for e in (1, 2, 3, 7)]))

        @pl.when(lax.rem(s, 2) == 1)
        def _():
            scatter_x(s, 0).wait_recv()
            for e in (1, 2, 3):
                scatter_y_on(s, e).wait_recv()
            finish_seq(s, total(dfar[s, :, chip_rows], [rsbuf[s, e] for e in (0, 4 + 1, 4 + 2, 4 + 3)]))

    def finish_seq(s, far):
        dn = dnear[s] + far.T
        xhat, rstd = layer_norm_parts(xraw[s].astype(F32))
        dx = rstd * (
            dn
            - jnp.mean(dn, -1, keepdims=True)
            - xhat * jnp.mean(dn * xhat, -1, keepdims=True)
        )
        ostage[s] = dx.astype(BF)

    def pair_swap(k):
        blk = pl.ds(k * CH, CH)
        return send(dxs.at[blk], dxr.at[blk], dx_s.at[k], dx_r.at[k], partner)

    def tile_copy(k, i):
        blk = pl.ds(k * CH, CH)
        hi = xlo if i < 4 else 1 - xlo
        return send(
            dbs.at[blk, :, block(hi, ring(z, i % 4))], dbr.at[i, blk], ds_s.at[k, i], ds_r.at[k, i], seq_peer(i)
        )

    def tiles_start(k):
        blk = pl.ds(k * CH, CH)
        dxs[blk] = dbias[blk, other_rows, :].astype(BF)
        pair_swap(k).start()

    def tiles_first(k):
        blk = pl.ds(k * CH, CH)
        pair_swap(k).wait_recv()
        dbs[blk] = (dbias[blk, my_rows, :] + dxr[blk].astype(F32)).astype(BF)
        for i in range(1, PEERS):
            tile_copy(k, i).start()

    def tiles_last(k):
        blk = pl.ds(k * CH, CH)
        for i in range(1, PEERS):
            tile_copy(k, i).wait_recv()
        return total(dbs[blk, :, my_cols], [dbr[i, blk] for i in range(1, PEERS)])

    scale = HD ** (-0.5)

    def prepare(s, t):
        gather_rest(s)
        x = xg[s]
        kt[t] = dot(wk[...], x, TT).astype(BF)
        vt[t] = dot(wv[...], x, TT).astype(BF)
        xq = xg[s, chip_rows, :]
        qf = dot(xq, wq[...]) * scale
        q_s[t] = qf.astype(BF)
        qT[t] = qf.T.astype(BF)
        gate = jax.nn.sigmoid(dot(xq, wg[...]))
        gt_s[t] = gate
        keep = keep_ref[p * SEQS + s].astype(F32)
        grad_in = (graw[s].astype(F32) * keep).astype(BF)
        dg = dot(grad_in, wo[...], NT)
        dg_s[t] = dg
        d_att = dg * gate
        do_s[t] = d_att.astype(BF)
        doT[t] = d_att.T.astype(BF)

    def scores(h, t):
        hs = slice(HD * h, HD * h + HD)
        logits = dot(q_s[t, :, hs], kt[t, hs, :]) + bias[h]
        return logits, dot(do_s[t, :, hs], vt[t, hs, :])

    def head(h, t, logits, d_prob, first):
        hs = slice(HD * h, HD * h + HD)
        top = jnp.max(logits, -1, keepdims=True)
        e = jnp.exp(logits - top)
        prob = e * (1.0 / jnp.sum(e, -1, keepdims=True))
        prob_half = prob.astype(BF)
        o_s[t, :, hs] = dot(prob_half, vt[t, hs, :], NT)
        d_log = prob * (d_prob - jnp.sum(prob * d_prob, -1, keepdims=True))
        if first:
            dbias[h] = d_log
        else:
            dbias[h] += d_log
        dlog_half = d_log.astype(BF)
        dq_s[t, :, hs] = (dot(dlog_half, kt[t, hs, :], NT) * scale).astype(BF)
        dkt[t, hs, :] = dot(qT[t, hs, :], dlog_half).astype(BF)
        dvt[t, hs, :] = dot(doT[t, hs, :], prob_half).astype(BF)

    def attention(items, first=None, hook=lambda n: None):
        held = scores(*items[0])
        for n, item in enumerate(items):
            ahead = scores(*items[n + 1]) if n + 1 < len(items) else None
            head(*item, *held, item[1] == first)
            hook(n)
            held = ahead

    def heads_of(t, *chunks):
        return [(h, t) for k in chunks for h in range(k * CH, k * CH + CH)]

    def finish(s, t):
        gate = gt_s[t]
        d_gate = (dg_s[t] * o_s[t] * gate * (1.0 - gate)).astype(BF)
        dfar[s] = (dot(wk[...], dkt[t]) + dot(wv[...], dvt[t])).astype(BF)
        return d_gate

    def near(s, t, d_gate):
        dnear[s] = dot(dq_s[t], wq[...], NT) + dot(d_gate, wg[...], NT)

    bias_arrive(0)
    prepare(0, 0)
    forward_copy(0).wait_recv()
    attention(heads_of(0, 0), 0)
    bias_second(3)
    bias_arrive(1)
    prepare(1, 1)
    forward_copy(1).wait_recv()
    gather_second(2)
    gather_first(4)
    attention(heads_of(0, 1) + heads_of(1, 0), 0)
    bias_arrive(2)
    gather_second(3)
    gather_first(5)
    attention(heads_of(1, 1), 0)
    forward_copy(2).wait_recv()
    gather_second(4)
    attention(heads_of(0, 2), 0)
    bias_arrive(3)
    attention(heads_of(1, 2), 0)
    forward_copy(3).wait_recv()
    gather_second(5)
    attention(heads_of(0, 3) + heads_of(1, 3), 0)
    for s in (0, 1):
        g0 = finish(s, s)
        scatter_first(s)
        near(s, s, g0)

    def seq_body(s, carry):
        prepare(s, 0)
        attention(heads_of(0, 0, 1, 2, 3))
        g0 = finish(s, 0)
        scatter_first(s)
        near(s, 0, g0)

        @pl.when(s == 2)
        def _():
            scatter_second(0)

        scatter_second(s - 1)

        @pl.when(s == 3)
        def _():
            scatter_last(0)

        @pl.when(s >= 3)
        def _():
            scatter_last(s - 2)

        return carry

    lax.fori_loop(2, SEQS - 1, seq_body, 0)

    last = SEQS - 1
    prepare(last, 1)

    def sending(n):
        if n % CH == CH - 1:
            k = n // CH
            tiles_start(k)
            if k > 0:
                tiles_first(k - 1)

    attention(heads_of(1, 0, 1, 2, 3), hook=sending)
    g0 = finish(last, 1)
    for i in (6, 5, 7, 2, 4, 1, 3):
        scatter_one(last, i).start()
    tiles_first(NCH - 1)
    near(last, 1, g0)
    scatter_second(last - 1)
    scatter_last(last - 2)

    def back_copy(i, at, n):
        return send(
            ostage.at[pl.ds(at, n), other_rows, :], orecv.at[pl.ds(at, n)], oo_s.at[i], oo_r.at[i], partner
        )

    backs = [back_copy(0, 0, last), back_copy(1, last, 1)]

    mean = stat[pl.ds(0, HALF, stride=8), :]
    rstd = stat[pl.ds(1, HALF, stride=8), :]
    coef_ref[...] = jnp.zeros_like(coef_ref)
    along = jnp.zeros((HALF, ROWS), F32)
    for k in range(NCH):
        tile = tiles_last(k)
        for i in range(CH):
            h = k * CH + i
            along = along + tile[i] * btmp[pl.ds(h, HALF, stride=8), :]
            coef_ref[pl.ds(h, HALF, stride=COEF), :] = tile[i] * rstd
        if k == 0:
            scatter_last(last - 1)
            backs[0].start()
    u = rstd * rstd * along * (1.0 / 128)
    coef_ref[pl.ds(HEADS, HALF, stride=COEF), :] = mean * u
    coef_ref[pl.ds(HEADS + 1, HALF, stride=COEF), :] = u

    for i in range(1, PEERS):
        scatter_one(last, i).wait_recv()
    finish_seq(last, total(dfar[last, :, chip_rows], [rsbuf[last, i] for i in range(1, PEERS)]))
    backs[1].start()
    out_ref[pl.ds(p * SEQS, SEQS)] = ostage[:, my_rows, :]
    for cp in backs:
        cp.wait_recv()
    out_ref[pl.ds(other * SEQS, SEQS)] = orecv[...]

    for cp in swaps:
        cp.wait_send()
    for cp in backs:
        cp.wait_send()
    for i in range(1, PEERS):
        scatter_one(last, i).wait_send()

    def drain_seq(s, carry):
        for e in (1, 2, 3, 4):
            gather_copy(s, e).wait_send()
        for e in (1, 2, 3):
            gather_on(s, e, True).wait_send()

        @pl.when(lax.rem(s, 2) == 0)
        def _():
            for e in (1, 2, 3):
                scatter_y(s, e, 0).wait_send()
                scatter_y(s, e, 1).wait_send()
            scatter_x_on(s).wait_send()

        @pl.when((lax.rem(s, 2) == 1) & (s < last))
        def _():
            for e in (0, 1, 2, 3):
                scatter_x(s, e).wait_send()
            for e in (1, 2, 3):
                scatter_y_on(s, e).wait_send()

        return carry

    lax.fori_loop(0, SEQS, drain_seq, 0)

    for k in range(NCH):
        forward_copy(k).wait_send()
        pair_swap(k).wait_send()
        for e in (1, 2, 3, 4):
            bias_copy(k, e).wait_send()
        for e in (1, 2, 3):
            bias_on(k, e).wait_send()
        for i in range(1, PEERS):
            tile_copy(k, i).wait_send()


def run_main(x, pair, g, wq, wk, wv, wg, wo, wpt, mask, keep):
    def vm(*shape, dt=BF):
        return pltpu.VMEM(shape, dt)

    dma = pltpu.SemaphoreType.DMA
    vmem = pl.BlockSpec(memory_space=pltpu.VMEM)
    smem = pl.BlockSpec(memory_space=pltpu.SMEM)
    return pl.pallas_call(
        main_kernel,
        out_shape=(
            jax.ShapeDtypeStruct(x.shape, BF),
            jax.ShapeDtypeStruct((HALF * COEF, ROWS), F32),
        ),
        in_specs=[vmem] * 10 + [smem],
        out_specs=[vmem, vmem],
        scratch_shapes=[
            vm(SEQS, ROWS, WIDTH),
            vm(SEQS, ROWS, WIDTH),
            vm(SEQS, RES, WIDTH),
            vm(HEADS, ROWS, RES, dt=F32),
            vm(HEADS, ROWS, RES, dt=F32),
            vm(HALF * 8, ROWS, dt=F32),
            vm(HALF * 8, ROWS, dt=F32),
            vm(2, WIDTH, RES),
            vm(2, WIDTH, RES),
            vm(2, ROWS, WIDTH),
            vm(2, ROWS, WIDTH),
            vm(2, WIDTH, ROWS),
            vm(2, WIDTH, ROWS),
            vm(2, ROWS, WIDTH, dt=F32),
            vm(2, ROWS, WIDTH),
            vm(2, WIDTH, RES),
            vm(2, WIDTH, RES),
            vm(2, ROWS, WIDTH, dt=F32),
            vm(2, ROWS, WIDTH, dt=F32),
            vm(SEQS, ROWS, WIDTH, dt=F32),
            vm(SEQS, WIDTH, RES),
            vm(SEQS, PEERS, WIDTH, ROWS),
            vm(SEQS, ROWS, WIDTH),
            vm(SEQS, HALF, WIDTH),
            vm(HEADS, HALF, RES),
            vm(HEADS, HALF, RES),
            vm(HEADS, HALF, RES),
            vm(PEERS, HEADS, HALF, ROWS),
            dma((2,)), dma((2,)),
            dma((SEQS, PEERS)), dma((SEQS, PEERS)),
            dma((SEQS, PEERS)), dma((SEQS, PEERS)),
            dma((NCH, PEERS)), dma((NCH, PEERS)),
            dma((NCH,)), dma((NCH,)),
            dma((NCH,)), dma((NCH,)),
            dma((NCH, PEERS)), dma((NCH, PEERS)),
            dma((2,)), dma((2,)),
        ],
        compiler_params=pltpu.CompilerParams(
            collective_id=0, has_side_effects=True, vmem_limit_bytes=56 * 2**20
        ),
        name="attention_backward",
    )(x, pair, g, wq, wk, wv, wg, wo, wpt, mask, keep)


PB = 16


def pair_kernel(pair_ref, coef_ref, wpt_ref, out_ref):
    w = wpt_ref[...]
    w_hi, w_lo = split(w - jnp.mean(w, -1, keepdims=True))
    one = jnp.ones((1, 128), BF)

    def rows(n):
        return jnp.zeros((n, 128), BF)

    first = jnp.concatenate(
        [jnp.concatenate([w_hi, one, rows(7)], 0), jnp.concatenate([rows(9), one, rows(6)], 0)], 1
    )
    second = jnp.concatenate([jnp.concatenate([w_lo, rows(8)], 0), rows(16)], 1)
    right = jnp.concatenate([first, first, first, second], 0)
    for i in range(PB):
        cf = coef_ref[i * COEF : (i + 1) * COEF, :]
        hi = cf.astype(BF)
        rest = cf - hi.astype(F32)
        mid, low = split(rest)
        both = lax.dot_general(
            jnp.concatenate([hi, mid, low, hi], 0), right, (((0,), (0,)), ((), ())),
            preferred_element_type=F32,
        )
        out_ref[i] = both[:, :128] - pair_ref[i].astype(F32) * both[:, 128:]


def run_pair(pair, coef, wpt):
    n = pair.shape[0]
    return pl.pallas_call(
        pair_kernel,
        grid=(n // PB,),
        out_shape=jax.ShapeDtypeStruct(pair.shape, F32),
        in_specs=[
            pl.BlockSpec((PB, 128, 128), lambda i: (i, 0, 0)),
            pl.BlockSpec((PB * COEF, 128), lambda i: (i, 0)),
            pl.BlockSpec((HEADS, 128), lambda i: (0, 0)),
        ],
        out_specs=pl.BlockSpec((PB, 128, 128), lambda i: (i, 0, 0)),
        name="pair_gradient",
    )(pair, coef, wpt)


def body(x, pair, g, wq, wk, wv, wg, wo, wp, mask, keep):
    wpt = wp.T
    dx, coef = run_main(x, pair, g, wq, wk, wv, wg, wo, wpt, mask.reshape(8, 128), keep)
    return dx, run_pair(pair, coef, wpt)


def solution(mesh):
    return jax.shard_map(
        body,
        mesh=mesh,
        in_specs=(
            P("seq", "res", None),
            P("res", "seq", None),
            P("seq", "res", None),
            P(),
            P(),
            P(),
            P(),
            P(),
            P(),
            P(),
            P("seq"),
        ),
        out_specs=(P("seq", "res", None), P("res", "seq", None)),
        check_vma=False,
    )
```

```python
import jax
import jax.numpy as jnp
from jax import lax
from jax.experimental import pallas as pl
from jax.experimental.pallas import tpu as pltpu
from jax.sharding import PartitionSpec as P

BF = jnp.bfloat16
F32 = jnp.float32
MESH = pl.DeviceIdType.MESH
EPS = 1e-05

SEQS = 6
ROWS = 128
HALF = 64
RES = 1024
WIDTH = 256
HEADS = 8
HD = 32
PEERS = 8
CH = 2
NCH = HEADS // CH
COEF = 16

NN = (((1,), (0,)), ((), ()))
NT = (((1,), (1,)), ((), ()))
TT = (((0,), (1,)), ((), ()))


def dot(a, b, dims=NN):
    return lax.dot_general(a, b, dims, preferred_element_type=F32)


def layer_norm_parts(x):
    mean = jnp.mean(x, -1, keepdims=True)
    cen = x - mean
    var = jnp.mean(cen * cen, -1, keepdims=True)
    rstd = lax.rsqrt(var + EPS)
    return cen * rstd, rstd


def split(x):
    hi = x.astype(BF)
    return hi, (x - hi.astype(F32)).astype(BF)


def main_kernel(
    x_ref, pair_ref, g_ref, wq, wk, wv, wg, wo, wpt_ref, mask_ref, keep_ref,
    out_ref, coef_ref,
    xraw, graw, xg, bias, dbias, btmp, stat, kt, vt, q_s, do_s, doT, qT, o_s, dq_s, dkt, dvt,
    dg_s, gt_s, dnear, dfar, rsbuf, ostage, orecv, dxs, dxr, dbs, dbr,
    sx_s, sx_r, ag_s, ag_r, rs_s, rs_r, bi_s, bi_r, bf_s, bf_r, dx_s, dx_r, ds_s, ds_r, oo_s, oo_r,
):
    sq = lax.axis_index("seq")
    rs = lax.axis_index("res")
    p = lax.rem(rs, 2)
    other = 1 - p
    y = lax.rem(lax.div(rs, 2), 4)
    xhi = lax.div(rs, 8)
    z = lax.rem(sq, 4)
    xlo = lax.div(sq, 4)
    partner = (sq, rs + 1 - 2 * p)
    x_peer = (sq, (1 - xhi) * 8 + y * 2 + p)
    lo_peer = ((1 - xlo) * 4 + z, rs)

    def ring(at, step):
        return lax.rem(at + step, 4)

    def y_peer(e):
        return (sq, xhi * 8 + ring(y, e) * 2 + p)

    def z_peer(e):
        return (xlo * 4 + ring(z, e), rs)

    def res_peer(i):
        hi = xhi if i < 4 else 1 - xhi
        return (sq, hi * 8 + ring(y, i % 4) * 2 + p)

    def seq_peer(i):
        hi = xlo if i < 4 else 1 - xlo
        return (hi * 4 + ring(z, i % 4), rs)

    def block(hi, at):
        return pl.ds(pl.multiple_of((hi * 4 + at) * ROWS, ROWS), ROWS)

    bar = pltpu.get_barrier_semaphore()
    for dev in [partner] + [f(i) for i in range(1, PEERS) for f in (res_peer, seq_peer)]:
        pl.semaphore_signal(bar, inc=1, device_id=dev, device_id_type=MESH)

    my_rows = pl.ds(pl.multiple_of(p * HALF, HALF), HALF)
    other_rows = pl.ds(pl.multiple_of(other * HALF, HALF), HALF)
    chip_rows = block(xhi, y)
    my_cols = block(xlo, z)

    def send(src, dst, s_sem, r_sem, dev):
        return pltpu.make_async_remote_copy(
            src_ref=src, dst_ref=dst, send_sem=s_sem, recv_sem=r_sem,
            device_id=dev, device_id_type=MESH,
        )

    def swap_copy(i, src, dst):
        return send(
            src.at[pl.ds(other * SEQS, SEQS)], dst.at[:, my_rows, :], sx_s.at[i], sx_r.at[i], partner
        )

    def gather_copy(s, e):
        blk = xg.at[s, chip_rows, :]
        return send(blk, blk, ag_s.at[s, e], ag_r.at[s, e], x_peer if e == 4 else y_peer(e))

    def gather_on(s, e, along_y):
        if along_y:
            blk, dev = xg.at[s, block(1 - xhi, y), :], y_peer(e)
        else:
            blk, dev = xg.at[s, block(xhi, ring(y, 4 - e)), :], x_peer
        return send(blk, blk, ag_s.at[s, 4 + e], ag_r.at[s, 4 + e], dev)

    def gather_one(s, i):
        blk = xg.at[s, chip_rows, :]
        return send(blk, blk, ag_s.at[s, i], ag_r.at[s, i], res_peer(i))

    def y_first(s):
        return (lax.rem(s, 2) == 1) & (s >= 3)

    def gather_first(s):
        for e in (4, 1, 2, 3):
            gather_copy(s, e).start()

    def gather_second(s):
        @pl.when(jnp.logical_not(y_first(s)))
        def _():
            gather_copy(s, 4).wait_recv()
            for e in (1, 2, 3):
                gather_on(s, e, True).start()

        @pl.when(y_first(s))
        def _():
            for e in (1, 2, 3):
                gather_copy(s, e).wait_recv()
                gather_on(s, e, False).start()

    def gather_rest(s):
        @pl.when(jnp.logical_not(y_first(s)))
        def _():
            for e in (1, 2, 3):
                gather_copy(s, e).wait_recv()

        @pl.when(y_first(s))
        def _():
            gather_copy(s, 4).wait_recv()

        for e in (1, 2, 3):
            gather_on(s, e, True).wait_recv()

    w = wpt_ref[...]
    w_hi, w_mid = split(w - jnp.mean(w, -1, keepdims=True))
    w_low = (w - jnp.mean(w, -1, keepdims=True) - w_hi.astype(F32) - w_mid.astype(F32)).astype(BF)
    left = jnp.concatenate([w_hi, w_mid, w_low, jnp.ones((8, 128), BF)], 0)
    ones = jnp.ones((8, WIDTH), BF)
    square = jnp.full((128, 128), 1.0 / 128, BF)
    top_row = lax.broadcasted_iota(jnp.int32, (8, 128), 0) == 0

    def pair_body(i, carry):
        xb = pair_ref[i]
        cen = xb.astype(F32) - dot(xb, square)
        s_hi, s_lo = split(cen * cen)
        proj = dot(left, xb, NT)
        var = dot(ones, jnp.concatenate([s_hi, s_lo], 1), NT) * (1.0 / 128)
        mean = proj[24:32] * (1.0 / 128)
        rstd = lax.rsqrt(var + EPS)
        at = pl.ds(pl.multiple_of(i * 8, 8), 8)
        btmp[at, :] = (proj[0:8] + (proj[8:16] + proj[16:24])) * rstd
        stat[at, :] = jnp.where(top_row, mean, rstd)
        return carry

    lax.fori_loop(0, HALF // 2, pair_body, 0, unroll=8)
    pl.semaphore_wait(bar, 2 * PEERS - 1)
    swaps = [swap_copy(0, x_ref, xraw), swap_copy(1, g_ref, graw)]
    for cp in swaps:
        cp.start()
    xraw[:, my_rows, :] = x_ref[pl.ds(p * SEQS, SEQS)]
    graw[:, my_rows, :] = g_ref[pl.ds(p * SEQS, SEQS)]

    lax.fori_loop(HALF // 2, HALF, pair_body, 0, unroll=8)

    def bias_copy(k, e):
        blk = bias.at[pl.ds(k * CH, CH), my_rows, my_cols]
        return send(blk, blk, bi_s.at[k, e], bi_r.at[k, e], lo_peer if e == 4 else z_peer(e))

    def bias_on(k, e):
        if k % 2 == 0:
            cols, dev = block(1 - xlo, z), z_peer(e)
        else:
            cols, dev = block(xlo, ring(z, 4 - e)), lo_peer
        blk = bias.at[pl.ds(k * CH, CH), my_rows, cols]
        return send(blk, blk, bi_s.at[k, 4 + e], bi_r.at[k, 4 + e], dev)

    def forward_copy(k):
        blk = bias.at[pl.ds(k * CH, CH), my_rows, :]
        return send(blk, blk, bf_s.at[k], bf_r.at[k], partner)

    usable = mask_ref[pl.ds(sq, 1), :] > 0
    for k in range(NCH):
        for h in range(k * CH, k * CH + CH):
            bias[h, my_rows, my_cols] = jnp.where(
                usable, btmp[pl.ds(h, HALF, stride=8), :], -1000000000.0
            )
        bias_copy(k, 4).start()

    def bias_first(k):
        for e in (1, 2, 3):
            bias_copy(k, e).start()

    bias_first(0)
    bias_first(1)

    def bias_second(k):
        if k % 2 == 0:
            bias_copy(k, 4).wait_recv()
            for e in (1, 2, 3):
                bias_on(k, e).start()
        else:
            for e in (1, 2, 3):
                bias_copy(k, e).wait_recv()
                bias_on(k, e).start()

    def bias_arrive(k):
        if k % 2 == 0:
            for e in (1, 2, 3):
                bias_copy(k, e).wait_recv()
        else:
            bias_copy(k, 4).wait_recv()
        for e in (1, 2, 3):
            bias_on(k, e).wait_recv()
        forward_copy(k).start()

    def norm(s):
        xhat, rstd = layer_norm_parts(xraw[s].astype(F32))
        xg[s, chip_rows, :] = xhat.astype(BF)

    def norm_body(s, carry):
        norm(s)
        return carry

    swaps[0].wait_recv()
    norm(0)
    for i in (1, 3, 4, 2, 5, 7, 6):
        gather_one(0, i).start()
    norm(1)
    gather_first(1)
    lax.fori_loop(2, SEQS, norm_body, 0)
    bias_second(0)
    bias_first(2)
    gather_first(2)
    swaps[1].wait_recv()

    def scatter_y(s, e, hi):
        row = xhi if hi == 0 else 1 - xhi
        i = e + 3 * hi
        return send(
            dfar.at[s, :, block(row, ring(y, e))], rsbuf.at[s, i], rs_s.at[s, i], rs_r.at[s, i], y_peer(e)
        )

    def scatter_x_on(s):
        return send(
            dfar.at[s, :, block(1 - xhi, y)], rsbuf.at[s, 7], rs_s.at[s, 7], rs_r.at[s, 7], x_peer
        )

    def scatter_x(s, e):
        return send(
            dfar.at[s, :, block(1 - xhi, ring(y, e))], rsbuf.at[s, e], rs_s.at[s, e], rs_r.at[s, e], x_peer
        )

    def scatter_y_on(s, e):
        return send(
            dfar.at[s, :, block(xhi, ring(y, e))], rsbuf.at[s, 4 + e], rs_s.at[s, 4 + e], rs_r.at[s, 4 + e],
            y_peer(e),
        )

    def scatter_one(s, i):
        hi = xhi if i < 4 else 1 - xhi
        return send(
            dfar.at[s, :, block(hi, ring(y, i % 4))], rsbuf.at[s, i], rs_s.at[s, i], rs_r.at[s, i], res_peer(i)
        )

    def total(first, parts):
        out = first.astype(F32)
        for part in parts:
            out = out + part.astype(F32)
        return out

    def scatter_first(s):
        @pl.when(lax.rem(s, 2) == 0)
        def _():
            for e in (1, 2, 3):
                scatter_y(s, e, 1).start()
            for e in (1, 2, 3):
                scatter_y(s, e, 0).start()

        @pl.when(lax.rem(s, 2) == 1)
        def _():
            for e in (1, 2, 3, 0):
                scatter_x(s, e).start()

    def scatter_second(s):
        @pl.when(lax.rem(s, 2) == 0)
        def _():
            for e in (1, 2, 3):
                scatter_y(s, e, 1).wait_recv()
            blk = block(1 - xhi, y)
            dfar[s, :, blk] = total(dfar[s, :, blk], [rsbuf[s, 3 + e] for e in (1, 2, 3)]).astype(BF)
            scatter_x_on(s).start()

        @pl.when(lax.rem(s, 2) == 1)
        def _():
            for e in (1, 2, 3):
                scatter_x(s, e).wait_recv()
                blk = block(xhi, ring(y, e))
                dfar[s, :, blk] = total(dfar[s, :, blk], [rsbuf[s, e]]).astype(BF)
                scatter_y_on(s, e).start()

    def scatter_last(s):
        @pl.when(lax.rem(s, 2) == 0)
        def _():
            for e in (1, 2, 3):
                scatter_y(s, e, 0).wait_recv()
            scatter_x_on(s).wait_recv()
            finish_seq(s, total(dfar[s, :, chip_rows], [rsbuf[s, e] for e in (1, 2, 3, 7)]))

        @pl.when(lax.rem(s, 2) == 1)
        def _():
            scatter_x(s, 0).wait_recv()
            for e in (1, 2, 3):
                scatter_y_on(s, e).wait_recv()
            finish_seq(s, total(dfar[s, :, chip_rows], [rsbuf[s, e] for e in (0, 4 + 1, 4 + 2, 4 + 3)]))

    def finish_seq(s, far):
        dn = dnear[s] + far.T
        xhat, rstd = layer_norm_parts(xraw[s].astype(F32))
        dx = rstd * (
            dn
            - jnp.mean(dn, -1, keepdims=True)
            - xhat * jnp.mean(dn * xhat, -1, keepdims=True)
        )
        ostage[s] = dx.astype(BF)

    def pair_swap(k):
        blk = pl.ds(k * CH, CH)
        return send(dxs.at[blk], dxr.at[blk], dx_s.at[k], dx_r.at[k], partner)

    def tile_copy(k, i):
        blk = pl.ds(k * CH, CH)
        hi = xlo if i < 4 else 1 - xlo
        return send(
            dbs.at[blk, :, block(hi, ring(z, i % 4))], dbr.at[i, blk], ds_s.at[k, i], ds_r.at[k, i], seq_peer(i)
        )

    def tiles_start(k):
        blk = pl.ds(k * CH, CH)
        dxs[blk] = dbias[blk, other_rows, :].astype(BF)
        pair_swap(k).start()

    def tiles_first(k):
        blk = pl.ds(k * CH, CH)
        pair_swap(k).wait_recv()
        dbs[blk] = (dbias[blk, my_rows, :] + dxr[blk].astype(F32)).astype(BF)
        for i in range(1, PEERS):
            tile_copy(k, i).start()

    def tiles_last(k):
        blk = pl.ds(k * CH, CH)
        for i in range(1, PEERS):
            tile_copy(k, i).wait_recv()
        return total(dbs[blk, :, my_cols], [dbr[i, blk] for i in range(1, PEERS)])

    scale = HD ** (-0.5)

    def prepare(s, t):
        x = xg[s]
        kt[t] = dot(wk[...], x, TT).astype(BF)
        vt[t] = dot(wv[...], x, TT).astype(BF)
        xq = xg[s, chip_rows, :]
        qf = dot(xq, wq[...]) * scale
        q_s[t] = qf.astype(BF)
        qT[t] = qf.T.astype(BF)
        gate = jax.nn.sigmoid(dot(xq, wg[...]))
        gt_s[t] = gate
        keep = keep_ref[p * SEQS + s].astype(F32)
        grad_in = (graw[s].astype(F32) * keep).astype(BF)
        dg = dot(grad_in, wo[...], NT)
        dg_s[t] = dg
        d_att = dg * gate
        do_s[t] = d_att.astype(BF)
        doT[t] = d_att.T.astype(BF)

    def scores(h, t):
        hs = slice(HD * h, HD * h + HD)
        logits = dot(q_s[t, :, hs], kt[t, hs, :]) + bias[h]
        return logits, dot(do_s[t, :, hs], vt[t, hs, :])

    def head(h, t, logits, d_prob, first):
        hs = slice(HD * h, HD * h + HD)
        top = jnp.max(logits, -1, keepdims=True)
        e = jnp.exp(logits - top)
        prob = e * (1.0 / jnp.sum(e, -1, keepdims=True))
        prob_half = prob.astype(BF)
        o_s[t, :, hs] = dot(prob_half, vt[t, hs, :], NT)
        d_log = prob * (d_prob - jnp.sum(prob * d_prob, -1, keepdims=True))
        if first:
            dbias[h] = d_log
        else:
            dbias[h] += d_log
        dlog_half = d_log.astype(BF)
        dq_s[t, :, hs] = (dot(dlog_half, kt[t, hs, :], NT) * scale).astype(BF)
        dkt[t, hs, :] = dot(qT[t, hs, :], dlog_half).astype(BF)
        dvt[t, hs, :] = dot(doT[t, hs, :], prob_half).astype(BF)

    def attention(items, first=None, hook=lambda n: None):
        held = scores(*items[0])
        for n, item in enumerate(items):
            ahead = scores(*items[n + 1]) if n + 1 < len(items) else None
            head(*item, *held, item[1] == first)
            hook(n)
            held = ahead

    def heads_of(t, *chunks):
        return [(h, t) for k in chunks for h in range(k * CH, k * CH + CH)]

    def finish(s, t):
        gate = gt_s[t]
        d_gate = (dg_s[t] * o_s[t] * gate * (1.0 - gate)).astype(BF)
        dfar[s] = (dot(wk[...], dkt[t]) + dot(wv[...], dvt[t])).astype(BF)
        return d_gate

    def near(s, t, d_gate):
        dnear[s] = dot(dq_s[t], wq[...], NT) + dot(d_gate, wg[...], NT)

    for i in range(1, PEERS):
        gather_one(0, i).wait_recv()
    prepare(0, 0)
    gather_second(1)
    gather_first(3)
    bias_second(1)
    bias_first(3)
    bias_second(2)
    bias_arrive(0)
    forward_copy(0).wait_recv()
    attention(heads_of(0, 0), 0)
    gather_second(2)
    gather_first(4)
    bias_second(3)
    bias_arrive(1)
    gather_rest(1)
    prepare(1, 1)
    forward_copy(1).wait_recv()
    gather_second(3)
    gather_first(5)
    attention(heads_of(0, 1) + heads_of(1, 0), 0)
    bias_arrive(2)
    attention(heads_of(1, 1), 0)
    forward_copy(2).wait_recv()
    gather_second(4)
    attention(heads_of(0, 2), 0)
    bias_arrive(3)
    attention(heads_of(1, 2), 0)
    forward_copy(3).wait_recv()
    gather_second(5)
    attention(heads_of(0, 3), 0)
    g0 = finish(0, 0)
    scatter_first(0)
    near(0, 0, g0)
    attention(heads_of(1, 3), 0)
    g0 = finish(1, 1)
    scatter_first(1)
    near(1, 1, g0)

    two = 4
    direct = (6, 5, 7, 2, 4, 1, 3)

    def seq_body(s, carry):
        gather_rest(s)
        prepare(s, 0)
        attention(heads_of(0, 0, 1, 2, 3))
        g0 = finish(s, 0)

        @pl.when(s < two)
        def _():
            scatter_first(s)

        @pl.when(s >= two)
        def _():
            for i in direct:
                scatter_one(s, i).start()

        near(s, 0, g0)

        @pl.when(s == 3)
        def _():
            scatter_second(0)
            scatter_second(1)

        @pl.when(s == 4)
        def _():
            scatter_second(2)
            scatter_last(0)
            scatter_last(1)

        return carry

    lax.fori_loop(2, SEQS - 1, seq_body, 0)

    last = SEQS - 1
    gather_rest(last)
    prepare(last, 1)

    def sending(n):
        if n % CH == CH - 1:
            k = n // CH
            tiles_start(k)
            if k > 0:
                tiles_first(k - 1)
            if k == 1:
                scatter_second(3)

    attention(heads_of(1, 0, 1, 2, 3), hook=sending)
    g0 = finish(last, 1)
    for i in direct:
        scatter_one(last, i).start()
    tiles_first(NCH - 1)
    near(last, 1, g0)
    scatter_last(2)
    scatter_last(3)

    def scatter_end(s):
        for i in range(1, PEERS):
            scatter_one(s, i).wait_recv()
        finish_seq(s, total(dfar[s, :, chip_rows], [rsbuf[s, i] for i in range(1, PEERS)]))

    def back_copy(i, at, n):
        return send(
            ostage.at[pl.ds(at, n), other_rows, :], orecv.at[pl.ds(at, n)], oo_s.at[i], oo_r.at[i], partner
        )

    backs = [back_copy(0, 0, last), back_copy(1, last, 1)]

    mean = stat[pl.ds(0, HALF, stride=8), :]
    rstd = stat[pl.ds(1, HALF, stride=8), :]
    coef_ref[...] = jnp.zeros_like(coef_ref)
    along = jnp.zeros((HALF, ROWS), F32)
    for k in range(NCH):
        tile = tiles_last(k)
        for i in range(CH):
            h = k * CH + i
            along = along + tile[i] * btmp[pl.ds(h, HALF, stride=8), :]
            coef_ref[pl.ds(h, HALF, stride=COEF), :] = tile[i] * rstd
        if k == 0:
            scatter_end(last - 1)
            backs[0].start()
    u = rstd * rstd * along * (1.0 / 128)
    coef_ref[pl.ds(HEADS, HALF, stride=COEF), :] = mean * u
    coef_ref[pl.ds(HEADS + 1, HALF, stride=COEF), :] = u

    scatter_end(last)
    backs[1].start()
    out_ref[pl.ds(p * SEQS, SEQS)] = ostage[:, my_rows, :]
    for cp in backs:
        cp.wait_recv()
    out_ref[pl.ds(other * SEQS, SEQS)] = orecv[...]

    for cp in swaps:
        cp.wait_send()
    for cp in backs:
        cp.wait_send()
    for i in range(1, PEERS):
        gather_one(0, i).wait_send()

    def drain_seq(s, carry):
        @pl.when(s > 0)
        def _():
            for e in (1, 2, 3, 4):
                gather_copy(s, e).wait_send()
            for e in (1, 2, 3):
                gather_on(s, e, True).wait_send()

        @pl.when(s >= two)
        def _():
            for i in range(1, PEERS):
                scatter_one(s, i).wait_send()

        @pl.when((lax.rem(s, 2) == 0) & (s < two))
        def _():
            for e in (1, 2, 3):
                scatter_y(s, e, 0).wait_send()
                scatter_y(s, e, 1).wait_send()
            scatter_x_on(s).wait_send()

        @pl.when((lax.rem(s, 2) == 1) & (s < two))
        def _():
            for e in (0, 1, 2, 3):
                scatter_x(s, e).wait_send()
            for e in (1, 2, 3):
                scatter_y_on(s, e).wait_send()

        return carry

    lax.fori_loop(0, SEQS, drain_seq, 0)

    for k in range(NCH):
        forward_copy(k).wait_send()
        pair_swap(k).wait_send()
        for e in (1, 2, 3, 4):
            bias_copy(k, e).wait_send()
        for e in (1, 2, 3):
            bias_on(k, e).wait_send()
        for i in range(1, PEERS):
            tile_copy(k, i).wait_send()


def run_main(x, pair, g, wq, wk, wv, wg, wo, wpt, mask, keep):
    def vm(*shape, dt=BF):
        return pltpu.VMEM(shape, dt)

    dma = pltpu.SemaphoreType.DMA
    vmem = pl.BlockSpec(memory_space=pltpu.VMEM)
    smem = pl.BlockSpec(memory_space=pltpu.SMEM)
    return pl.pallas_call(
        main_kernel,
        out_shape=(
            jax.ShapeDtypeStruct(x.shape, BF),
            jax.ShapeDtypeStruct((HALF * COEF, ROWS), F32),
        ),
        in_specs=[vmem] * 10 + [smem],
        out_specs=[vmem, vmem],
        scratch_shapes=[
            vm(SEQS, ROWS, WIDTH),
            vm(SEQS, ROWS, WIDTH),
            vm(SEQS, RES, WIDTH),
            vm(HEADS, ROWS, RES, dt=F32),
            vm(HEADS, ROWS, RES, dt=F32),
            vm(HALF * 8, ROWS, dt=F32),
            vm(HALF * 8, ROWS, dt=F32),
            vm(2, WIDTH, RES),
            vm(2, WIDTH, RES),
            vm(2, ROWS, WIDTH),
            vm(2, ROWS, WIDTH),
            vm(2, WIDTH, ROWS),
            vm(2, WIDTH, ROWS),
            vm(2, ROWS, WIDTH, dt=F32),
            vm(2, ROWS, WIDTH),
            vm(2, WIDTH, RES),
            vm(2, WIDTH, RES),
            vm(2, ROWS, WIDTH, dt=F32),
            vm(2, ROWS, WIDTH, dt=F32),
            vm(SEQS, ROWS, WIDTH, dt=F32),
            vm(SEQS, WIDTH, RES),
            vm(SEQS, PEERS, WIDTH, ROWS),
            vm(SEQS, ROWS, WIDTH),
            vm(SEQS, HALF, WIDTH),
            vm(HEADS, HALF, RES),
            vm(HEADS, HALF, RES),
            vm(HEADS, HALF, RES),
            vm(PEERS, HEADS, HALF, ROWS),
            dma((2,)), dma((2,)),
            dma((SEQS, PEERS)), dma((SEQS, PEERS)),
            dma((SEQS, PEERS)), dma((SEQS, PEERS)),
            dma((NCH, PEERS)), dma((NCH, PEERS)),
            dma((NCH,)), dma((NCH,)),
            dma((NCH,)), dma((NCH,)),
            dma((NCH, PEERS)), dma((NCH, PEERS)),
            dma((2,)), dma((2,)),
        ],
        compiler_params=pltpu.CompilerParams(
            collective_id=0, has_side_effects=True, vmem_limit_bytes=56 * 2**20
        ),
        name="attention_backward",
    )(x, pair, g, wq, wk, wv, wg, wo, wpt, mask, keep)


PB = 16


def pair_kernel(pair_ref, coef_ref, wpt_ref, out_ref):
    w = wpt_ref[...]
    w_hi, w_lo = split(w - jnp.mean(w, -1, keepdims=True))
    one = jnp.ones((1, 128), BF)

    def rows(n):
        return jnp.zeros((n, 128), BF)

    first = jnp.concatenate(
        [jnp.concatenate([w_hi, one, rows(7)], 0), jnp.concatenate([rows(9), one, rows(6)], 0)], 1
    )
    second = jnp.concatenate([jnp.concatenate([w_lo, rows(8)], 0), rows(16)], 1)
    right = jnp.concatenate([first, first, first, second], 0)
    for i in range(PB):
        cf = coef_ref[i * COEF : (i + 1) * COEF, :]
        hi = cf.astype(BF)
        rest = cf - hi.astype(F32)
        mid, low = split(rest)
        both = lax.dot_general(
            jnp.concatenate([hi, mid, low, hi], 0), right, (((0,), (0,)), ((), ())),
            preferred_element_type=F32,
        )
        out_ref[i] = both[:, :128] - pair_ref[i].astype(F32) * both[:, 128:]


def run_pair(pair, coef, wpt):
    n = pair.shape[0]
    return pl.pallas_call(
        pair_kernel,
        grid=(n // PB,),
        out_shape=jax.ShapeDtypeStruct(pair.shape, F32),
        in_specs=[
            pl.BlockSpec((PB, 128, 128), lambda i: (i, 0, 0)),
            pl.BlockSpec((PB * COEF, 128), lambda i: (i, 0)),
            pl.BlockSpec((HEADS, 128), lambda i: (0, 0)),
        ],
        out_specs=pl.BlockSpec((PB, 128, 128), lambda i: (i, 0, 0)),
        name="pair_gradient",
    )(pair, coef, wpt)


def body(x, pair, g, wq, wk, wv, wg, wo, wp, mask, keep):
    wpt = wp.T
    dx, coef = run_main(x, pair, g, wq, wk, wv, wg, wo, wpt, mask.reshape(8, 128), keep)
    return dx, run_pair(pair, coef, wpt)


def solution(mesh):
    return jax.shard_map(
        body,
        mesh=mesh,
        in_specs=(
            P("seq", "res", None),
            P("res", "seq", None),
            P("seq", "res", None),
            P(),
            P(),
            P(),
            P(),
            P(),
            P(),
            P(),
            P("seq"),
        ),
        out_specs=(P("seq", "res", None), P("res", "seq", None)),
        check_vma=False,
    )
```

```python
import jax
import jax.numpy as jnp
from jax import lax
from jax.experimental import pallas as pl
from jax.experimental.pallas import tpu as pltpu
from jax.sharding import PartitionSpec as P

BF = jnp.bfloat16
F32 = jnp.float32
MESH = pl.DeviceIdType.MESH
EPS = 1e-05

SEQS = 6
ROWS = 128
HALF = 64
RES = 1024
WIDTH = 256
HEADS = 8
HD = 32
PEERS = 8
CH = 2
NCH = HEADS // CH
COEF = 16

NN = (((1,), (0,)), ((), ()))
NT = (((1,), (1,)), ((), ()))
TT = (((0,), (1,)), ((), ()))


def dot(a, b, dims=NN):
    return lax.dot_general(a, b, dims, preferred_element_type=F32)


def layer_norm_parts(x):
    mean = jnp.mean(x, -1, keepdims=True)
    cen = x - mean
    var = jnp.mean(cen * cen, -1, keepdims=True)
    rstd = lax.rsqrt(var + EPS)
    return cen * rstd, rstd


def split(x):
    hi = x.astype(BF)
    return hi, (x - hi.astype(F32)).astype(BF)


def main_kernel(
    x_ref, pair_ref, g_ref, wq, wk, wv, wg, wo, wpt_ref, mask_ref, keep_ref,
    out_ref, coef_ref,
    xraw, graw, xg, bias, dbias, btmp, stat, kt, vt, q_s, do_s, doT, qT, o_s, dq_s, dkt, dvt,
    dg_s, gt_s, dnear, dfar, rsbuf, ostage, orecv, dxs, dxr, dbs, dbr,
    sx_s, sx_r, ag_s, ag_r, rs_s, rs_r, bi_s, bi_r, bf_s, bf_r, dx_s, dx_r, ds_s, ds_r, oo_s, oo_r,
):
    sq = lax.axis_index("seq")
    rs = lax.axis_index("res")
    p = lax.rem(rs, 2)
    other = 1 - p
    y = lax.rem(lax.div(rs, 2), 4)
    xhi = lax.div(rs, 8)
    z = lax.rem(sq, 4)
    xlo = lax.div(sq, 4)
    partner = (sq, rs + 1 - 2 * p)
    x_peer = (sq, (1 - xhi) * 8 + y * 2 + p)
    lo_peer = ((1 - xlo) * 4 + z, rs)

    def ring(at, step):
        return lax.rem(at + step, 4)

    def y_peer(e):
        return (sq, xhi * 8 + ring(y, e) * 2 + p)

    def z_peer(e):
        return (xlo * 4 + ring(z, e), rs)

    def res_peer(i):
        hi = xhi if i < 4 else 1 - xhi
        return (sq, hi * 8 + ring(y, i % 4) * 2 + p)

    def seq_peer(i):
        hi = xlo if i < 4 else 1 - xlo
        return (hi * 4 + ring(z, i % 4), rs)

    def block(hi, at):
        return pl.ds(pl.multiple_of((hi * 4 + at) * ROWS, ROWS), ROWS)

    bar = pltpu.get_barrier_semaphore()
    for dev in [partner] + [f(i) for i in range(1, PEERS) for f in (res_peer, seq_peer)]:
        pl.semaphore_signal(bar, inc=1, device_id=dev, device_id_type=MESH)

    my_rows = pl.ds(pl.multiple_of(p * HALF, HALF), HALF)
    other_rows = pl.ds(pl.multiple_of(other * HALF, HALF), HALF)
    chip_rows = block(xhi, y)
    my_cols = block(xlo, z)

    def send(src, dst, s_sem, r_sem, dev):
        return pltpu.make_async_remote_copy(
            src_ref=src, dst_ref=dst, send_sem=s_sem, recv_sem=r_sem,
            device_id=dev, device_id_type=MESH,
        )

    def swap_copy(i, src, dst):
        return send(
            src.at[pl.ds(other * SEQS, SEQS)], dst.at[:, my_rows, :], sx_s.at[i], sx_r.at[i], partner
        )

    def gather_copy(s, e):
        blk = xg.at[s, chip_rows, :]
        return send(blk, blk, ag_s.at[s, e], ag_r.at[s, e], x_peer if e == 4 else y_peer(e))

    def gather_on(s, e, along_y):
        if along_y:
            blk, dev = xg.at[s, block(1 - xhi, y), :], y_peer(e)
        else:
            blk, dev = xg.at[s, block(xhi, ring(y, 4 - e)), :], x_peer
        return send(blk, blk, ag_s.at[s, 4 + e], ag_r.at[s, 4 + e], dev)

    def gather_one(s, i):
        blk = xg.at[s, chip_rows, :]
        return send(blk, blk, ag_s.at[s, i], ag_r.at[s, i], res_peer(i))

    def y_first(s):
        return (lax.rem(s, 2) == 1) & (s >= 3)

    def gather_first(s):
        for e in (4, 1, 2, 3):
            gather_copy(s, e).start()

    def gather_second(s):
        @pl.when(jnp.logical_not(y_first(s)))
        def _():
            gather_copy(s, 4).wait_recv()
            for e in (1, 2, 3):
                gather_on(s, e, True).start()

        @pl.when(y_first(s))
        def _():
            for e in (1, 2, 3):
                gather_copy(s, e).wait_recv()
                gather_on(s, e, False).start()

    def gather_rest(s):
        @pl.when(jnp.logical_not(y_first(s)))
        def _():
            for e in (1, 2, 3):
                gather_copy(s, e).wait_recv()

        @pl.when(y_first(s))
        def _():
            gather_copy(s, 4).wait_recv()

        for e in (1, 2, 3):
            gather_on(s, e, True).wait_recv()

    w = wpt_ref[...]
    w_hi, w_mid = split(w - jnp.mean(w, -1, keepdims=True))
    w_low = (w - jnp.mean(w, -1, keepdims=True) - w_hi.astype(F32) - w_mid.astype(F32)).astype(BF)
    left = jnp.concatenate([w_hi, w_mid, w_low, jnp.ones((8, 128), BF)], 0)
    ones = jnp.ones((8, WIDTH), BF)
    square = jnp.full((128, 128), 1.0 / 128, BF)
    top_row = lax.broadcasted_iota(jnp.int32, (8, 128), 0) == 0

    def pair_body(i, carry):
        xb = pair_ref[i]
        cen = xb.astype(F32) - dot(xb, square)
        s_hi, s_lo = split(cen * cen)
        proj = dot(left, xb, NT)
        var = dot(ones, jnp.concatenate([s_hi, s_lo], 1), NT) * (1.0 / 128)
        mean = proj[24:32] * (1.0 / 128)
        rstd = lax.rsqrt(var + EPS)
        at = pl.ds(pl.multiple_of(i * 8, 8), 8)
        btmp[at, :] = (proj[0:8] + (proj[8:16] + proj[16:24])) * rstd
        stat[at, :] = jnp.where(top_row, mean, rstd)
        return carry

    lax.fori_loop(0, HALF // 2, pair_body, 0, unroll=8)
    pl.semaphore_wait(bar, 2 * PEERS - 1)
    swaps = [swap_copy(0, x_ref, xraw), swap_copy(1, g_ref, graw)]
    for cp in swaps:
        cp.start()
    xraw[:, my_rows, :] = x_ref[pl.ds(p * SEQS, SEQS)]
    graw[:, my_rows, :] = g_ref[pl.ds(p * SEQS, SEQS)]

    lax.fori_loop(HALF // 2, HALF, pair_body, 0, unroll=8)

    def bias_copy(k, e):
        blk = bias.at[pl.ds(k * CH, CH), my_rows, my_cols]
        return send(blk, blk, bi_s.at[k, e], bi_r.at[k, e], lo_peer if e == 4 else z_peer(e))

    def bias_on(k, e):
        if k % 2 == 0 or k == 3:
            cols, dev = block(1 - xlo, z), z_peer(e)
        else:
            cols, dev = block(xlo, ring(z, 4 - e)), lo_peer
        blk = bias.at[pl.ds(k * CH, CH), my_rows, cols]
        return send(blk, blk, bi_s.at[k, 4 + e], bi_r.at[k, 4 + e], dev)

    def forward_copy(k):
        blk = bias.at[pl.ds(k * CH, CH), my_rows, :]
        return send(blk, blk, bf_s.at[k], bf_r.at[k], partner)

    usable = mask_ref[pl.ds(sq, 1), :] > 0
    for k in range(NCH):
        for h in range(k * CH, k * CH + CH):
            bias[h, my_rows, my_cols] = jnp.where(
                usable, btmp[pl.ds(h, HALF, stride=8), :], -1000000000.0
            )
        bias_copy(k, 4).start()

    def bias_first(k):
        for e in (1, 2, 3):
            bias_copy(k, e).start()

    bias_first(0)
    bias_first(1)

    def bias_second(k):
        if k % 2 == 0 or k == 3:
            bias_copy(k, 4).wait_recv()
            for e in (1, 2, 3):
                bias_on(k, e).start()
        else:
            for e in (1, 2, 3):
                bias_copy(k, e).wait_recv()
                bias_on(k, e).start()

    def bias_arrive(k):
        if k % 2 == 0 or k == 3:
            for e in (1, 2, 3):
                bias_copy(k, e).wait_recv()
        else:
            bias_copy(k, 4).wait_recv()
        for e in (1, 2, 3):
            bias_on(k, e).wait_recv()
        forward_copy(k).start()

    def norm(s):
        xhat, rstd = layer_norm_parts(xraw[s].astype(F32))
        xg[s, chip_rows, :] = xhat.astype(BF)

    def norm_body(s, carry):
        norm(s)
        return carry

    swaps[0].wait_recv()
    norm(0)
    for i in (1, 3, 4, 2, 5, 7, 6):
        gather_one(0, i).start()
    norm(1)
    gather_first(1)
    lax.fori_loop(2, SEQS, norm_body, 0)
    bias_second(0)
    bias_first(2)
    gather_first(2)
    swaps[1].wait_recv()

    def scatter_y(s, e, hi):
        row = xhi if hi == 0 else 1 - xhi
        i = e + 3 * hi
        return send(
            dfar.at[s, :, block(row, ring(y, e))], rsbuf.at[s, i], rs_s.at[s, i], rs_r.at[s, i], y_peer(e)
        )

    def scatter_x_on(s):
        return send(
            dfar.at[s, :, block(1 - xhi, y)], rsbuf.at[s, 7], rs_s.at[s, 7], rs_r.at[s, 7], x_peer
        )

    def scatter_x(s, e):
        return send(
            dfar.at[s, :, block(1 - xhi, ring(y, e))], rsbuf.at[s, e], rs_s.at[s, e], rs_r.at[s, e], x_peer
        )

    def scatter_y_on(s, e):
        return send(
            dfar.at[s, :, block(xhi, ring(y, e))], rsbuf.at[s, 4 + e], rs_s.at[s, 4 + e], rs_r.at[s, 4 + e],
            y_peer(e),
        )

    def scatter_one(s, i):
        hi = xhi if i < 4 else 1 - xhi
        return send(
            dfar.at[s, :, block(hi, ring(y, i % 4))], rsbuf.at[s, i], rs_s.at[s, i], rs_r.at[s, i], res_peer(i)
        )

    def total(first, parts):
        out = first.astype(F32)
        for part in parts:
            out = out + part.astype(F32)
        return out

    def scatter_first(s):
        @pl.when(lax.rem(s, 2) == 0)
        def _():
            for e in (1, 2, 3):
                scatter_y(s, e, 1).start()
            for e in (1, 2, 3):
                scatter_y(s, e, 0).start()

        @pl.when(lax.rem(s, 2) == 1)
        def _():
            for e in (1, 2, 3, 0):
                scatter_x(s, e).start()

    def scatter_second(s):
        @pl.when(lax.rem(s, 2) == 0)
        def _():
            for e in (1, 2, 3):
                scatter_y(s, e, 1).wait_recv()
            blk = block(1 - xhi, y)
            dfar[s, :, blk] = total(dfar[s, :, blk], [rsbuf[s, 3 + e] for e in (1, 2, 3)]).astype(BF)
            scatter_x_on(s).start()

        @pl.when(lax.rem(s, 2) == 1)
        def _():
            for e in (1, 2, 3):
                scatter_x(s, e).wait_recv()
                blk = block(xhi, ring(y, e))
                dfar[s, :, blk] = total(dfar[s, :, blk], [rsbuf[s, e]]).astype(BF)
                scatter_y_on(s, e).start()

    def scatter_last(s):
        @pl.when(lax.rem(s, 2) == 0)
        def _():
            for e in (1, 2, 3):
                scatter_y(s, e, 0).wait_recv()
            scatter_x_on(s).wait_recv()
            finish_seq(s, total(dfar[s, :, chip_rows], [rsbuf[s, e] for e in (1, 2, 3, 7)]))

        @pl.when(lax.rem(s, 2) == 1)
        def _():
            scatter_x(s, 0).wait_recv()
            for e in (1, 2, 3):
                scatter_y_on(s, e).wait_recv()
            finish_seq(s, total(dfar[s, :, chip_rows], [rsbuf[s, e] for e in (0, 4 + 1, 4 + 2, 4 + 3)]))

    def finish_seq(s, far):
        dn = dnear[s] + far.T
        xhat, rstd = layer_norm_parts(xraw[s].astype(F32))
        dx = rstd * (
            dn
            - jnp.mean(dn, -1, keepdims=True)
            - xhat * jnp.mean(dn * xhat, -1, keepdims=True)
        )
        ostage[s] = dx.astype(BF)

    def pair_swap(k):
        blk = pl.ds(k * CH, CH)
        return send(dxs.at[blk], dxr.at[blk], dx_s.at[k], dx_r.at[k], partner)

    def tile_copy(k, i):
        blk = pl.ds(k * CH, CH)
        hi = xlo if i < 4 else 1 - xlo
        return send(
            dbs.at[blk, :, block(hi, ring(z, i % 4))], dbr.at[i, blk], ds_s.at[k, i], ds_r.at[k, i], seq_peer(i)
        )

    def tile_z(k, e, i):
        blk = pl.ds(k * CH, CH)
        hi = xlo if i < 4 else 1 - xlo
        return send(
            dbs.at[blk, :, block(hi, ring(z, e))], dbr.at[i, blk], ds_s.at[k, i], ds_r.at[k, i], z_peer(e)
        )

    def tile_lo(k):
        blk = pl.ds(k * CH, CH)
        return send(
            dbs.at[blk, :, block(1 - xlo, z)], dbr.at[4, blk], ds_s.at[k, 4], ds_r.at[k, 4], lo_peer
        )

    def tiles_start(k):
        blk = pl.ds(k * CH, CH)
        dxs[blk] = dbias[blk, other_rows, :].astype(BF)
        pair_swap(k).start()

    def tiles_first(k):
        blk = pl.ds(k * CH, CH)
        pair_swap(k).wait_recv()
        dbs[blk] = (dbias[blk, my_rows, :] + dxr[blk].astype(F32)).astype(BF)
        if k == NCH - 1:
            for i in range(1, PEERS):
                tile_copy(k, i).start()
        else:
            for e in (1, 2, 3):
                tile_z(k, e, e + 4).start()
            for e in (1, 2, 3):
                tile_z(k, e, e).start()

    def tiles_second(k):
        blk = pl.ds(k * CH, CH)
        for e in (1, 2, 3):
            tile_z(k, e, e + 4).wait_recv()
        cols = block(1 - xlo, z)
        dbs[blk, :, cols] = total(dbs[blk, :, cols], [dbr[i, blk] for i in (5, 6, 7)]).astype(BF)
        tile_lo(k).start()

    def tiles_last(k):
        blk = pl.ds(k * CH, CH)
        if k == NCH - 1:
            for i in range(1, PEERS):
                tile_copy(k, i).wait_recv()
            return total(dbs[blk, :, my_cols], [dbr[i, blk] for i in range(1, PEERS)])
        for e in (1, 2, 3):
            tile_z(k, e, e).wait_recv()
        tile_lo(k).wait_recv()
        return total(dbs[blk, :, my_cols], [dbr[i, blk] for i in (1, 2, 3, 4)])

    scale = HD ** (-0.5)

    def prepare(s, t):
        x = xg[s]
        kt[t] = dot(wk[...], x, TT).astype(BF)
        vt[t] = dot(wv[...], x, TT).astype(BF)
        xq = xg[s, chip_rows, :]
        qf = dot(xq, wq[...]) * scale
        q_s[t] = qf.astype(BF)
        qT[t] = qf.T.astype(BF)
        gate = jax.nn.sigmoid(dot(xq, wg[...]))
        gt_s[t] = gate
        keep = keep_ref[p * SEQS + s].astype(F32)
        grad_in = (graw[s].astype(F32) * keep).astype(BF)
        dg = dot(grad_in, wo[...], NT)
        dg_s[t] = dg
        d_att = dg * gate
        do_s[t] = d_att.astype(BF)
        doT[t] = d_att.T.astype(BF)

    def scores(h, t):
        hs = slice(HD * h, HD * h + HD)
        logits = dot(q_s[t, :, hs], kt[t, hs, :]) + bias[h]
        return logits, dot(do_s[t, :, hs], vt[t, hs, :])

    def head(h, t, logits, d_prob, first):
        hs = slice(HD * h, HD * h + HD)
        top = jnp.max(logits, -1, keepdims=True)
        e = jnp.exp(logits - top)
        prob = e * (1.0 / jnp.sum(e, -1, keepdims=True))
        prob_half = prob.astype(BF)
        o_s[t, :, hs] = dot(prob_half, vt[t, hs, :], NT)
        d_log = prob * (d_prob - jnp.sum(prob * d_prob, -1, keepdims=True))
        if first:
            dbias[h] = d_log
        else:
            dbias[h] += d_log
        dlog_half = d_log.astype(BF)
        dq_s[t, :, hs] = (dot(dlog_half, kt[t, hs, :], NT) * scale).astype(BF)
        dkt[t, hs, :] = dot(qT[t, hs, :], dlog_half).astype(BF)
        dvt[t, hs, :] = dot(doT[t, hs, :], prob_half).astype(BF)

    def attention(items, first=None, hook=lambda n: None):
        held = scores(*items[0])
        for n, item in enumerate(items):
            ahead = scores(*items[n + 1]) if n + 1 < len(items) else None
            head(*item, *held, item[1] == first)
            hook(n)
            held = ahead

    def heads_of(t, *chunks):
        return [(h, t) for k in chunks for h in range(k * CH, k * CH + CH)]

    def finish(s, t):
        gate = gt_s[t]
        d_gate = (dg_s[t] * o_s[t] * gate * (1.0 - gate)).astype(BF)
        dfar[s] = (dot(wk[...], dkt[t]) + dot(wv[...], dvt[t])).astype(BF)
        return d_gate

    def near(s, t, d_gate):
        dnear[s] = dot(dq_s[t], wq[...], NT) + dot(d_gate, wg[...], NT)

    for i in range(1, PEERS):
        gather_one(0, i).wait_recv()
    prepare(0, 0)
    gather_second(1)
    gather_first(3)
    bias_second(1)
    bias_first(3)
    bias_second(2)
    bias_arrive(0)
    forward_copy(0).wait_recv()
    attention(heads_of(0, 0), 0)
    gather_second(2)
    gather_first(4)
    bias_second(3)
    bias_arrive(1)
    gather_rest(1)
    prepare(1, 1)
    forward_copy(1).wait_recv()
    gather_second(3)
    gather_first(5)
    attention(heads_of(0, 1) + heads_of(1, 0), 0)
    bias_arrive(2)
    attention(heads_of(1, 1), 0)
    forward_copy(2).wait_recv()
    gather_second(4)
    attention(heads_of(0, 2), 0)
    bias_arrive(3)
    attention(heads_of(1, 2), 0)
    forward_copy(3).wait_recv()
    gather_second(5)
    attention(heads_of(0, 3), 0)
    g0 = finish(0, 0)
    scatter_first(0)
    near(0, 0, g0)
    attention(heads_of(1, 3), 0)
    g0 = finish(1, 1)
    scatter_first(1)
    near(1, 1, g0)

    two = 4
    direct = (6, 5, 7, 2, 4, 1, 3)

    def seq_body(s, carry):
        gather_rest(s)
        prepare(s, 0)
        attention(heads_of(0, 0, 1, 2, 3))
        g0 = finish(s, 0)

        @pl.when(s < two)
        def _():
            scatter_first(s)

        @pl.when(s >= two)
        def _():
            for i in direct:
                scatter_one(s, i).start()

        near(s, 0, g0)

        @pl.when(s == 3)
        def _():
            scatter_second(0)
            scatter_second(1)

        @pl.when(s == 4)
        def _():
            scatter_second(2)
            scatter_last(0)
            scatter_last(1)

        return carry

    lax.fori_loop(2, SEQS - 1, seq_body, 0)

    last = SEQS - 1
    gather_rest(last)
    prepare(last, 1)

    def sending(n):
        if n % CH == CH - 1:
            k = n // CH
            tiles_start(k)
            if k > 0:
                tiles_first(k - 1)
            if k == 2:
                scatter_second(3)
            if k == 3:
                tiles_second(0)

    attention(heads_of(1, 0, 1, 2, 3), hook=sending)
    g0 = finish(last, 1)
    for i in direct:
        scatter_one(last, i).start()
    tiles_first(NCH - 1)
    near(last, 1, g0)
    tiles_second(1)
    scatter_last(2)
    scatter_last(3)
    tiles_second(2)

    def scatter_end(s):
        for i in range(1, PEERS):
            scatter_one(s, i).wait_recv()
        finish_seq(s, total(dfar[s, :, chip_rows], [rsbuf[s, i] for i in range(1, PEERS)]))

    def back_copy(i, at, n):
        return send(
            ostage.at[pl.ds(at, n), other_rows, :], orecv.at[pl.ds(at, n)], oo_s.at[i], oo_r.at[i], partner
        )

    backs = [back_copy(0, 0, last), back_copy(1, last, 1)]

    mean = stat[pl.ds(0, HALF, stride=8), :]
    rstd = stat[pl.ds(1, HALF, stride=8), :]
    coef_ref[...] = jnp.zeros_like(coef_ref)
    along = jnp.zeros((HALF, ROWS), F32)
    for k in range(NCH):
        tile = tiles_last(k)
        for i in range(CH):
            h = k * CH + i
            along = along + tile[i] * btmp[pl.ds(h, HALF, stride=8), :]
            coef_ref[pl.ds(h, HALF, stride=COEF), :] = tile[i] * rstd
        if k == 0:
            scatter_end(last - 1)
            backs[0].start()
    u = rstd * rstd * along * (1.0 / 128)
    coef_ref[pl.ds(HEADS, HALF, stride=COEF), :] = mean * u
    coef_ref[pl.ds(HEADS + 1, HALF, stride=COEF), :] = u

    scatter_end(last)
    backs[1].start()
    out_ref[pl.ds(p * SEQS, SEQS)] = ostage[:, my_rows, :]
    for cp in backs:
        cp.wait_recv()
    out_ref[pl.ds(other * SEQS, SEQS)] = orecv[...]

    for cp in swaps:
        cp.wait_send()
    for cp in backs:
        cp.wait_send()
    for i in range(1, PEERS):
        gather_one(0, i).wait_send()

    def drain_seq(s, carry):
        @pl.when(s > 0)
        def _():
            for e in (1, 2, 3, 4):
                gather_copy(s, e).wait_send()
            for e in (1, 2, 3):
                gather_on(s, e, True).wait_send()

        @pl.when(s >= two)
        def _():
            for i in range(1, PEERS):
                scatter_one(s, i).wait_send()

        @pl.when((lax.rem(s, 2) == 0) & (s < two))
        def _():
            for e in (1, 2, 3):
                scatter_y(s, e, 0).wait_send()
                scatter_y(s, e, 1).wait_send()
            scatter_x_on(s).wait_send()

        @pl.when((lax.rem(s, 2) == 1) & (s < two))
        def _():
            for e in (0, 1, 2, 3):
                scatter_x(s, e).wait_send()
            for e in (1, 2, 3):
                scatter_y_on(s, e).wait_send()

        return carry

    lax.fori_loop(0, SEQS, drain_seq, 0)

    for k in range(NCH):
        forward_copy(k).wait_send()
        pair_swap(k).wait_send()
        for e in (1, 2, 3, 4):
            bias_copy(k, e).wait_send()
        for e in (1, 2, 3):
            bias_on(k, e).wait_send()
        if k == NCH - 1:
            for i in range(1, PEERS):
                tile_copy(k, i).wait_send()
        else:
            for e in (1, 2, 3):
                tile_z(k, e, e).wait_send()
                tile_z(k, e, e + 4).wait_send()
            tile_lo(k).wait_send()


def run_main(x, pair, g, wq, wk, wv, wg, wo, wpt, mask, keep):
    def vm(*shape, dt=BF):
        return pltpu.VMEM(shape, dt)

    dma = pltpu.SemaphoreType.DMA
    vmem = pl.BlockSpec(memory_space=pltpu.VMEM)
    smem = pl.BlockSpec(memory_space=pltpu.SMEM)
    return pl.pallas_call(
        main_kernel,
        out_shape=(
            jax.ShapeDtypeStruct(x.shape, BF),
            jax.ShapeDtypeStruct((HALF * COEF, ROWS), F32),
        ),
        in_specs=[vmem] * 10 + [smem],
        out_specs=[vmem, vmem],
        scratch_shapes=[
            vm(SEQS, ROWS, WIDTH),
            vm(SEQS, ROWS, WIDTH),
            vm(SEQS, RES, WIDTH),
            vm(HEADS, ROWS, RES, dt=F32),
            vm(HEADS, ROWS, RES, dt=F32),
            vm(HALF * 8, ROWS, dt=F32),
            vm(HALF * 8, ROWS, dt=F32),
            vm(2, WIDTH, RES),
            vm(2, WIDTH, RES),
            vm(2, ROWS, WIDTH),
            vm(2, ROWS, WIDTH),
            vm(2, WIDTH, ROWS),
            vm(2, WIDTH, ROWS),
            vm(2, ROWS, WIDTH, dt=F32),
            vm(2, ROWS, WIDTH),
            vm(2, WIDTH, RES),
            vm(2, WIDTH, RES),
            vm(2, ROWS, WIDTH, dt=F32),
            vm(2, ROWS, WIDTH, dt=F32),
            vm(SEQS, ROWS, WIDTH, dt=F32),
            vm(SEQS, WIDTH, RES),
            vm(SEQS, PEERS, WIDTH, ROWS),
            vm(SEQS, ROWS, WIDTH),
            vm(SEQS, HALF, WIDTH),
            vm(HEADS, HALF, RES),
            vm(HEADS, HALF, RES),
            vm(HEADS, HALF, RES),
            vm(PEERS, HEADS, HALF, ROWS),
            dma((2,)), dma((2,)),
            dma((SEQS, PEERS)), dma((SEQS, PEERS)),
            dma((SEQS, PEERS)), dma((SEQS, PEERS)),
            dma((NCH, PEERS)), dma((NCH, PEERS)),
            dma((NCH,)), dma((NCH,)),
            dma((NCH,)), dma((NCH,)),
            dma((NCH, PEERS)), dma((NCH, PEERS)),
            dma((2,)), dma((2,)),
        ],
        compiler_params=pltpu.CompilerParams(
            collective_id=0, has_side_effects=True, vmem_limit_bytes=56 * 2**20
        ),
        name="attention_backward",
    )(x, pair, g, wq, wk, wv, wg, wo, wpt, mask, keep)


PB = 16


def pair_kernel(pair_ref, coef_ref, wpt_ref, out_ref):
    w = wpt_ref[...]
    w_hi, w_lo = split(w - jnp.mean(w, -1, keepdims=True))
    one = jnp.ones((1, 128), BF)

    def rows(n):
        return jnp.zeros((n, 128), BF)

    first = jnp.concatenate(
        [jnp.concatenate([w_hi, one, rows(7)], 0), jnp.concatenate([rows(9), one, rows(6)], 0)], 1
    )
    second = jnp.concatenate([jnp.concatenate([w_lo, rows(8)], 0), rows(16)], 1)
    right = jnp.concatenate([first, first, first, second], 0)
    for i in range(PB):
        cf = coef_ref[i * COEF : (i + 1) * COEF, :]
        hi = cf.astype(BF)
        rest = cf - hi.astype(F32)
        mid, low = split(rest)
        both = lax.dot_general(
            jnp.concatenate([hi, mid, low, hi], 0), right, (((0,), (0,)), ((), ())),
            preferred_element_type=F32,
        )
        out_ref[i] = both[:, :128] - pair_ref[i].astype(F32) * both[:, 128:]


def run_pair(pair, coef, wpt):
    n = pair.shape[0]
    return pl.pallas_call(
        pair_kernel,
        grid=(n // PB,),
        out_shape=jax.ShapeDtypeStruct(pair.shape, F32),
        in_specs=[
            pl.BlockSpec((PB, 128, 128), lambda i: (i, 0, 0)),
            pl.BlockSpec((PB * COEF, 128), lambda i: (i, 0)),
            pl.BlockSpec((HEADS, 128), lambda i: (0, 0)),
        ],
        out_specs=pl.BlockSpec((PB, 128, 128), lambda i: (i, 0, 0)),
        name="pair_gradient",
    )(pair, coef, wpt)


def body(x, pair, g, wq, wk, wv, wg, wo, wp, mask, keep):
    wpt = wp.T
    dx, coef = run_main(x, pair, g, wq, wk, wv, wg, wo, wpt, mask.reshape(8, 128), keep)
    return dx, run_pair(pair, coef, wpt)


def solution(mesh):
    return jax.shard_map(
        body,
        mesh=mesh,
        in_specs=(
            P("seq", "res", None),
            P("res", "seq", None),
            P("seq", "res", None),
            P(),
            P(),
            P(),
            P(),
            P(),
            P(),
            P(),
            P("seq"),
        ),
        out_specs=(P("seq", "res", None), P("res", "seq", None)),
        check_vma=False,
    )
```

```python
import jax
import jax.numpy as jnp
from jax import lax
from jax.experimental import pallas as pl
from jax.experimental.pallas import tpu as pltpu
from jax.sharding import PartitionSpec as P

BF = jnp.bfloat16
F32 = jnp.float32
MESH = pl.DeviceIdType.MESH
EPS = 1e-05

SEQS = 6
ROWS = 128
HALF = 64
RES = 1024
WIDTH = 256
HEADS = 8
HD = 32
PEERS = 8
CH = 2
NCH = HEADS // CH
COEF = 16

NN = (((1,), (0,)), ((), ()))
NT = (((1,), (1,)), ((), ()))
TT = (((0,), (1,)), ((), ()))


def dot(a, b, dims=NN):
    return lax.dot_general(a, b, dims, preferred_element_type=F32)


def layer_norm_parts(x):
    mean = jnp.mean(x, -1, keepdims=True)
    cen = x - mean
    var = jnp.mean(cen * cen, -1, keepdims=True)
    rstd = lax.rsqrt(var + EPS)
    return cen * rstd, rstd


def split(x):
    hi = x.astype(BF)
    return hi, (x - hi.astype(F32)).astype(BF)


def main_kernel(
    x_ref, pair_ref, g_ref, wq, wk, wv, wg, wo, wpt_ref, mask_ref, keep_ref,
    out_ref, coef_ref,
    xraw, graw, xg, bias, dbias, btmp, stat, kt, vt, q_s, do_s, doT, qT, o_s, dq_s, dkt, dvt,
    dg_s, gt_s, dnear, dfar, rsbuf, ostage, orecv, dxs, dxr, dbs, dbr,
    sx_s, sx_r, ag_s, ag_r, rs_s, rs_r, bi_s, bi_r, bf_s, bf_r, dx_s, dx_r, ds_s, ds_r, oo_s, oo_r,
):
    sq = lax.axis_index("seq")
    rs = lax.axis_index("res")
    p = lax.rem(rs, 2)
    other = 1 - p
    y = lax.rem(lax.div(rs, 2), 4)
    xhi = lax.div(rs, 8)
    z = lax.rem(sq, 4)
    xlo = lax.div(sq, 4)
    partner = (sq, rs + 1 - 2 * p)
    x_peer = (sq, (1 - xhi) * 8 + y * 2 + p)
    lo_peer = ((1 - xlo) * 4 + z, rs)

    def ring(at, step):
        return lax.rem(at + step, 4)

    def y_peer(e):
        return (sq, xhi * 8 + ring(y, e) * 2 + p)

    def z_peer(e):
        return (xlo * 4 + ring(z, e), rs)

    def res_peer(i):
        hi = xhi if i < 4 else 1 - xhi
        return (sq, hi * 8 + ring(y, i % 4) * 2 + p)

    def seq_peer(i):
        hi = xlo if i < 4 else 1 - xlo
        return (hi * 4 + ring(z, i % 4), rs)

    def block(hi, at):
        return pl.ds(pl.multiple_of((hi * 4 + at) * ROWS, ROWS), ROWS)

    bar = pltpu.get_barrier_semaphore()
    for dev in [partner] + [f(i) for i in range(1, PEERS) for f in (res_peer, seq_peer)]:
        pl.semaphore_signal(bar, inc=1, device_id=dev, device_id_type=MESH)

    my_rows = pl.ds(pl.multiple_of(p * HALF, HALF), HALF)
    other_rows = pl.ds(pl.multiple_of(other * HALF, HALF), HALF)
    chip_rows = block(xhi, y)
    my_cols = block(xlo, z)

    def send(src, dst, s_sem, r_sem, dev):
        return pltpu.make_async_remote_copy(
            src_ref=src, dst_ref=dst, send_sem=s_sem, recv_sem=r_sem,
            device_id=dev, device_id_type=MESH,
        )

    def swap_copy(i, src, dst):
        return send(
            src.at[pl.ds(other * SEQS, SEQS)], dst.at[:, my_rows, :], sx_s.at[i], sx_r.at[i], partner
        )

    def gather_copy(s, e):
        blk = xg.at[s, chip_rows, :]
        return send(blk, blk, ag_s.at[s, e], ag_r.at[s, e], x_peer if e == 4 else y_peer(e))

    def gather_on(s, e, along_y):
        if along_y:
            blk, dev = xg.at[s, block(1 - xhi, y), :], y_peer(e)
        else:
            blk, dev = xg.at[s, block(xhi, ring(y, 4 - e)), :], x_peer
        return send(blk, blk, ag_s.at[s, 4 + e], ag_r.at[s, 4 + e], dev)

    def gather_one(s, i):
        blk = xg.at[s, chip_rows, :]
        return send(blk, blk, ag_s.at[s, i], ag_r.at[s, i], res_peer(i))

    def y_first(s):
        return (lax.rem(s, 2) == 1) & (s >= 3)

    def gather_first(s):
        for e in (4, 1, 2, 3):
            gather_copy(s, e).start()

    def gather_second(s):
        @pl.when(jnp.logical_not(y_first(s)))
        def _():
            gather_copy(s, 4).wait_recv()
            for e in (1, 2, 3):
                gather_on(s, e, True).start()

        @pl.when(y_first(s))
        def _():
            for e in (1, 2, 3):
                gather_copy(s, e).wait_recv()
                gather_on(s, e, False).start()

    def gather_rest(s):
        @pl.when(jnp.logical_not(y_first(s)))
        def _():
            for e in (1, 2, 3):
                gather_copy(s, e).wait_recv()

        @pl.when(y_first(s))
        def _():
            gather_copy(s, 4).wait_recv()

        for e in (1, 2, 3):
            gather_on(s, e, True).wait_recv()

    w = wpt_ref[...]
    w_hi, w_mid = split(w - jnp.mean(w, -1, keepdims=True))
    w_low = (w - jnp.mean(w, -1, keepdims=True) - w_hi.astype(F32) - w_mid.astype(F32)).astype(BF)
    left = jnp.concatenate([w_hi, w_mid, w_low, jnp.ones((8, 128), BF)], 0)
    ones = jnp.ones((8, WIDTH), BF)
    square = jnp.full((128, 128), 1.0 / 128, BF)
    top_row = lax.broadcasted_iota(jnp.int32, (8, 128), 0) == 0

    def pair_body(i, carry):
        xb = pair_ref[i]
        cen = xb.astype(F32) - dot(xb, square)
        s_hi, s_lo = split(cen * cen)
        proj = dot(left, xb, NT)
        var = dot(ones, jnp.concatenate([s_hi, s_lo], 1), NT) * (1.0 / 128)
        mean = proj[24:32] * (1.0 / 128)
        rstd = lax.rsqrt(var + EPS)
        at = pl.ds(pl.multiple_of(i * 8, 8), 8)
        btmp[at, :] = (proj[0:8] + (proj[8:16] + proj[16:24])) * rstd
        stat[at, :] = jnp.where(top_row, mean, rstd)
        return carry

    lax.fori_loop(0, HALF // 2, pair_body, 0, unroll=8)
    pl.semaphore_wait(bar, 2 * PEERS - 1)
    swaps = [swap_copy(0, x_ref, xraw), swap_copy(1, g_ref, graw)]
    for cp in swaps:
        cp.start()
    xraw[:, my_rows, :] = x_ref[pl.ds(p * SEQS, SEQS)]
    graw[:, my_rows, :] = g_ref[pl.ds(p * SEQS, SEQS)]

    lax.fori_loop(HALF // 2, HALF, pair_body, 0, unroll=8)

    def bias_copy(k, e):
        blk = bias.at[pl.ds(k * CH, CH), my_rows, my_cols]
        return send(blk, blk, bi_s.at[k, e], bi_r.at[k, e], lo_peer if e == 4 else z_peer(e))

    def bias_on(k, e):
        if k % 2 == 0 or k == 3:
            cols, dev = block(1 - xlo, z), z_peer(e)
        else:
            cols, dev = block(xlo, ring(z, 4 - e)), lo_peer
        blk = bias.at[pl.ds(k * CH, CH), my_rows, cols]
        return send(blk, blk, bi_s.at[k, 4 + e], bi_r.at[k, 4 + e], dev)

    def forward_copy(k):
        blk = bias.at[pl.ds(k * CH, CH), my_rows, :]
        return send(blk, blk, bf_s.at[k], bf_r.at[k], partner)

    usable = mask_ref[pl.ds(sq, 1), :] > 0
    for k in range(NCH):
        for h in range(k * CH, k * CH + CH):
            bias[h, my_rows, my_cols] = jnp.where(
                usable, btmp[pl.ds(h, HALF, stride=8), :], -1000000000.0
            )
        bias_copy(k, 4).start()

    def bias_first(k):
        for e in (1, 2, 3):
            bias_copy(k, e).start()

    bias_first(0)
    bias_first(1)

    def bias_second(k):
        if k % 2 == 0 or k == 3:
            bias_copy(k, 4).wait_recv()
            for e in (1, 2, 3):
                bias_on(k, e).start()
        else:
            for e in (1, 2, 3):
                bias_copy(k, e).wait_recv()
                bias_on(k, e).start()

    def bias_arrive(k):
        if k % 2 == 0 or k == 3:
            for e in (1, 2, 3):
                bias_copy(k, e).wait_recv()
        else:
            bias_copy(k, 4).wait_recv()
        for e in (1, 2, 3):
            bias_on(k, e).wait_recv()
        forward_copy(k).start()

    def norm(s):
        xhat, rstd = layer_norm_parts(xraw[s].astype(F32))
        xg[s, chip_rows, :] = xhat.astype(BF)

    def norm_body(s, carry):
        norm(s)
        return carry

    swaps[0].wait_recv()
    norm(0)
    for i in (1, 3, 4, 2, 5, 7, 6):
        gather_one(0, i).start()
    norm(1)
    gather_first(1)
    lax.fori_loop(2, SEQS, norm_body, 0)
    bias_second(0)
    bias_first(2)
    gather_first(2)
    swaps[1].wait_recv()

    def scatter_y(s, e, hi):
        row = xhi if hi == 0 else 1 - xhi
        i = e + 3 * hi
        return send(
            dfar.at[s, :, block(row, ring(y, e))], rsbuf.at[s, i], rs_s.at[s, i], rs_r.at[s, i], y_peer(e)
        )

    def scatter_x_on(s):
        return send(
            dfar.at[s, :, block(1 - xhi, y)], rsbuf.at[s, 7], rs_s.at[s, 7], rs_r.at[s, 7], x_peer
        )

    def scatter_x(s, e):
        return send(
            dfar.at[s, :, block(1 - xhi, ring(y, e))], rsbuf.at[s, e], rs_s.at[s, e], rs_r.at[s, e], x_peer
        )

    def scatter_y_on(s, e):
        return send(
            dfar.at[s, :, block(xhi, ring(y, e))], rsbuf.at[s, 4 + e], rs_s.at[s, 4 + e], rs_r.at[s, 4 + e],
            y_peer(e),
        )

    def scatter_one(s, i):
        hi = xhi if i < 4 else 1 - xhi
        return send(
            dfar.at[s, :, block(hi, ring(y, i % 4))], rsbuf.at[s, i], rs_s.at[s, i], rs_r.at[s, i], res_peer(i)
        )

    def total(first, parts):
        out = first.astype(F32)
        for part in parts:
            out = out + part.astype(F32)
        return out

    def scatter_first(s):
        @pl.when(lax.rem(s, 2) == 0)
        def _():
            for e in (1, 2, 3):
                scatter_y(s, e, 1).start()
            for e in (1, 2, 3):
                scatter_y(s, e, 0).start()

        @pl.when(lax.rem(s, 2) == 1)
        def _():
            for e in (1, 2, 3, 0):
                scatter_x(s, e).start()

    def scatter_second(s):
        @pl.when(lax.rem(s, 2) == 0)
        def _():
            for e in (1, 2, 3):
                scatter_y(s, e, 1).wait_recv()
            blk = block(1 - xhi, y)
            dfar[s, :, blk] = total(dfar[s, :, blk], [rsbuf[s, 3 + e] for e in (1, 2, 3)]).astype(BF)
            scatter_x_on(s).start()

        @pl.when(lax.rem(s, 2) == 1)
        def _():
            for e in (1, 2, 3):
                scatter_x(s, e).wait_recv()
                blk = block(xhi, ring(y, e))
                dfar[s, :, blk] = total(dfar[s, :, blk], [rsbuf[s, e]]).astype(BF)
                scatter_y_on(s, e).start()

    def scatter_last(s):
        @pl.when(lax.rem(s, 2) == 0)
        def _():
            for e in (1, 2, 3):
                scatter_y(s, e, 0).wait_recv()
            scatter_x_on(s).wait_recv()
            finish_seq(s, total(dfar[s, :, chip_rows], [rsbuf[s, e] for e in (1, 2, 3, 7)]))

        @pl.when(lax.rem(s, 2) == 1)
        def _():
            scatter_x(s, 0).wait_recv()
            for e in (1, 2, 3):
                scatter_y_on(s, e).wait_recv()
            finish_seq(s, total(dfar[s, :, chip_rows], [rsbuf[s, e] for e in (0, 4 + 1, 4 + 2, 4 + 3)]))

    def finish_seq(s, far):
        dn = dnear[s] + far.T
        xhat, rstd = layer_norm_parts(xraw[s].astype(F32))
        dx = rstd * (
            dn
            - jnp.mean(dn, -1, keepdims=True)
            - xhat * jnp.mean(dn * xhat, -1, keepdims=True)
        )
        ostage[s] = dx.astype(BF)

    def pair_swap(k):
        blk = pl.ds(k * CH, CH)
        return send(dxs.at[blk], dxr.at[blk], dx_s.at[k], dx_r.at[k], partner)

    def tile_copy(k, i):
        blk = pl.ds(k * CH, CH)
        hi = xlo if i < 4 else 1 - xlo
        return send(
            dbs.at[blk, :, block(hi, ring(z, i % 4))], dbr.at[i, blk], ds_s.at[k, i], ds_r.at[k, i], seq_peer(i)
        )

    def tile_z(k, e, i):
        blk = pl.ds(k * CH, CH)
        hi = xlo if i < 4 else 1 - xlo
        return send(
            dbs.at[blk, :, block(hi, ring(z, e))], dbr.at[i, blk], ds_s.at[k, i], ds_r.at[k, i], z_peer(e)
        )

    def tile_lo(k):
        blk = pl.ds(k * CH, CH)
        return send(
            dbs.at[blk, :, block(1 - xlo, z)], dbr.at[4, blk], ds_s.at[k, 4], ds_r.at[k, 4], lo_peer
        )

    def tiles_start(k):
        blk = pl.ds(k * CH, CH)
        dxs[blk] = dbias[blk, other_rows, :].astype(BF)
        pair_swap(k).start()

    def tiles_first(k):
        blk = pl.ds(k * CH, CH)
        pair_swap(k).wait_recv()
        dbs[blk] = (dbias[blk, my_rows, :] + dxr[blk].astype(F32)).astype(BF)
        if k == NCH - 1:
            for i in range(1, PEERS):
                tile_copy(k, i).start()
        else:
            for e in (1, 2, 3):
                tile_z(k, e, e + 4).start()
            for e in (1, 2, 3):
                tile_z(k, e, e).start()

    def tiles_second(k):
        blk = pl.ds(k * CH, CH)
        for e in (1, 2, 3):
            tile_z(k, e, e + 4).wait_recv()
        cols = block(1 - xlo, z)
        dbs[blk, :, cols] = total(dbs[blk, :, cols], [dbr[i, blk] for i in (5, 6, 7)]).astype(BF)
        tile_lo(k).start()

    def tiles_last(k):
        blk = pl.ds(k * CH, CH)
        if k == NCH - 1:
            for i in range(1, PEERS):
                tile_copy(k, i).wait_recv()
            return total(dbs[blk, :, my_cols], [dbr[i, blk] for i in range(1, PEERS)])
        for e in (1, 2, 3):
            tile_z(k, e, e).wait_recv()
        tile_lo(k).wait_recv()
        return total(dbs[blk, :, my_cols], [dbr[i, blk] for i in (1, 2, 3, 4)])

    scale = HD ** (-0.5)

    def prepare(s, t):
        x = xg[s]
        kt[t] = dot(wk[...], x, TT).astype(BF)
        vt[t] = dot(wv[...], x, TT).astype(BF)
        xq = xg[s, chip_rows, :]
        qf = dot(xq, wq[...]) * scale
        q_s[t] = qf.astype(BF)
        qT[t] = qf.T.astype(BF)
        gate = jax.nn.sigmoid(dot(xq, wg[...]))
        gt_s[t] = gate
        keep = keep_ref[p * SEQS + s].astype(F32)
        grad_in = (graw[s].astype(F32) * keep).astype(BF)
        dg = dot(grad_in, wo[...], NT)
        dg_s[t] = dg
        d_att = dg * gate
        do_s[t] = d_att.astype(BF)
        doT[t] = d_att.T.astype(BF)

    def scores(h, t):
        hs = slice(HD * h, HD * h + HD)
        logits = dot(q_s[t, :, hs], kt[t, hs, :]) + bias[h]
        return logits, dot(do_s[t, :, hs], vt[t, hs, :])

    def head(h, t, logits, d_prob, first):
        hs = slice(HD * h, HD * h + HD)
        top = jnp.max(logits, -1, keepdims=True)
        e = jnp.exp(logits - top)
        prob = e * (1.0 / jnp.sum(e, -1, keepdims=True))
        prob_half = prob.astype(BF)
        o_s[t, :, hs] = dot(prob_half, vt[t, hs, :], NT)
        d_log = prob * (d_prob - jnp.sum(prob * d_prob, -1, keepdims=True))
        if first:
            dbias[h] = d_log
        else:
            dbias[h] += d_log
        dlog_half = d_log.astype(BF)
        dq_s[t, :, hs] = (dot(dlog_half, kt[t, hs, :], NT) * scale).astype(BF)
        dkt[t, hs, :] = dot(qT[t, hs, :], dlog_half).astype(BF)
        dvt[t, hs, :] = dot(doT[t, hs, :], prob_half).astype(BF)

    def attention(items, first=None, hook=lambda n: None):
        held = scores(*items[0])
        for n, item in enumerate(items):
            ahead = scores(*items[n + 1]) if n + 1 < len(items) else None
            head(*item, *held, item[1] == first)
            hook(n)
            held = ahead

    def heads_of(t, *chunks):
        return [(h, t) for k in chunks for h in range(k * CH, k * CH + CH)]

    def finish(s, t):
        gate = gt_s[t]
        d_gate = (dg_s[t] * o_s[t] * gate * (1.0 - gate)).astype(BF)
        dfar[s] = (dot(wk[...], dkt[t]) + dot(wv[...], dvt[t])).astype(BF)
        return d_gate

    def near(s, t, d_gate):
        dnear[s] = dot(dq_s[t], wq[...], NT) + dot(d_gate, wg[...], NT)

    for i in range(1, PEERS):
        gather_one(0, i).wait_recv()
    prepare(0, 0)
    gather_second(1)
    gather_first(3)
    bias_second(1)
    bias_first(3)
    bias_second(2)
    bias_arrive(0)
    forward_copy(0).wait_recv()
    attention(heads_of(0, 0), 0)
    gather_second(2)
    gather_first(4)
    bias_second(3)
    bias_arrive(1)
    gather_rest(1)
    prepare(1, 1)
    forward_copy(1).wait_recv()
    gather_second(3)
    gather_first(5)
    attention(heads_of(0, 1) + heads_of(1, 0), 0)
    bias_arrive(2)
    attention(heads_of(1, 1), 0)
    forward_copy(2).wait_recv()
    gather_second(4)
    attention(heads_of(0, 2), 0)
    bias_arrive(3)
    attention(heads_of(1, 2), 0)
    forward_copy(3).wait_recv()
    gather_second(5)
    attention(heads_of(0, 3), 0)
    g0 = finish(0, 0)
    scatter_first(0)
    near(0, 0, g0)
    attention(heads_of(1, 3), 0)
    g0 = finish(1, 1)
    scatter_first(1)
    near(1, 1, g0)

    two = 4
    direct = (6, 5, 7, 2, 4, 1, 3)

    def seq_body(s, carry):
        gather_rest(s)
        prepare(s, 0)
        attention(heads_of(0, 0, 1, 2, 3))
        g0 = finish(s, 0)

        @pl.when(s < two)
        def _():
            scatter_first(s)

        @pl.when(s >= two)
        def _():
            for i in direct:
                scatter_one(s, i).start()

        near(s, 0, g0)

        @pl.when(s == 3)
        def _():
            scatter_second(0)
            scatter_second(1)

        @pl.when(s == 4)
        def _():
            scatter_second(2)
            scatter_last(0)
            scatter_last(1)

        return carry

    lax.fori_loop(2, SEQS - 1, seq_body, 0)

    last = SEQS - 1
    gather_rest(last)
    prepare(last, 1)

    def sending(n):
        if n % CH == CH - 1:
            k = n // CH
            tiles_start(k)
            if k > 0:
                tiles_first(k - 1)
            if k == 2:
                scatter_second(3)
            if k == 3:
                tiles_second(0)

    attention(heads_of(1, 0, 1, 2, 3), hook=sending)
    g0 = finish(last, 1)
    for i in direct:
        scatter_one(last, i).start()
    tiles_first(NCH - 1)
    near(last, 1, g0)
    tiles_second(1)
    scatter_last(2)
    scatter_last(3)
    tiles_second(2)

    def scatter_end(s):
        for i in range(1, PEERS):
            scatter_one(s, i).wait_recv()
        finish_seq(s, total(dfar[s, :, chip_rows], [rsbuf[s, i] for i in range(1, PEERS)]))

    def back_copy(i, at, n):
        return send(
            ostage.at[pl.ds(at, n), other_rows, :], orecv.at[pl.ds(at, n)], oo_s.at[i], oo_r.at[i], partner
        )

    backs = [back_copy(0, 0, last), back_copy(1, last, 1)]

    mean = stat[pl.ds(0, HALF, stride=8), :]
    rstd = stat[pl.ds(1, HALF, stride=8), :]
    coef_ref[...] = jnp.zeros_like(coef_ref)
    along = jnp.zeros((HALF, ROWS), F32)
    for k in range(NCH):
        tile = tiles_last(k)
        for i in range(CH):
            h = k * CH + i
            along = along + tile[i] * btmp[pl.ds(h, HALF, stride=8), :]
            coef_ref[pl.ds(h, HALF, stride=COEF), :] = tile[i] * rstd
        if k == 0:
            scatter_end(last - 1)
            backs[0].start()
    u = rstd * rstd * along * (1.0 / 128)
    coef_ref[pl.ds(HEADS, HALF, stride=COEF), :] = mean * u
    coef_ref[pl.ds(HEADS + 1, HALF, stride=COEF), :] = u

    scatter_end(last)
    backs[1].start()
    out_ref[pl.ds(p * SEQS, SEQS)] = ostage[:, my_rows, :]
    for cp in backs:
        cp.wait_recv()
    out_ref[pl.ds(other * SEQS, SEQS)] = orecv[...]

    for cp in swaps:
        cp.wait_send()
    for cp in backs:
        cp.wait_send()
    for i in range(1, PEERS):
        gather_one(0, i).wait_send()

    def drain_seq(s, carry):
        @pl.when(s > 0)
        def _():
            for e in (1, 2, 3, 4):
                gather_copy(s, e).wait_send()
            for e in (1, 2, 3):
                gather_on(s, e, True).wait_send()

        @pl.when(s >= two)
        def _():
            for i in range(1, PEERS):
                scatter_one(s, i).wait_send()

        @pl.when((lax.rem(s, 2) == 0) & (s < two))
        def _():
            for e in (1, 2, 3):
                scatter_y(s, e, 0).wait_send()
                scatter_y(s, e, 1).wait_send()
            scatter_x_on(s).wait_send()

        @pl.when((lax.rem(s, 2) == 1) & (s < two))
        def _():
            for e in (0, 1, 2, 3):
                scatter_x(s, e).wait_send()
            for e in (1, 2, 3):
                scatter_y_on(s, e).wait_send()

        return carry

    lax.fori_loop(0, SEQS, drain_seq, 0)

    for k in range(NCH):
        forward_copy(k).wait_send()
        pair_swap(k).wait_send()
        for e in (1, 2, 3, 4):
            bias_copy(k, e).wait_send()
        for e in (1, 2, 3):
            bias_on(k, e).wait_send()
        if k == NCH - 1:
            for i in range(1, PEERS):
                tile_copy(k, i).wait_send()
        else:
            for e in (1, 2, 3):
                tile_z(k, e, e).wait_send()
                tile_z(k, e, e + 4).wait_send()
            tile_lo(k).wait_send()


def run_main(x, pair, g, wq, wk, wv, wg, wo, wpt, mask, keep):
    def vm(*shape, dt=BF):
        return pltpu.VMEM(shape, dt)

    dma = pltpu.SemaphoreType.DMA
    vmem = pl.BlockSpec(memory_space=pltpu.VMEM)
    smem = pl.BlockSpec(memory_space=pltpu.SMEM)
    return pl.pallas_call(
        main_kernel,
        out_shape=(
            jax.ShapeDtypeStruct(x.shape, BF),
            jax.ShapeDtypeStruct(((HALF + 1) * COEF, ROWS), F32),
        ),
        in_specs=[vmem] * 10 + [smem],
        out_specs=[vmem, vmem],
        scratch_shapes=[
            vm(SEQS, ROWS, WIDTH),
            vm(SEQS, ROWS, WIDTH),
            vm(SEQS, RES, WIDTH),
            vm(HEADS, ROWS, RES, dt=F32),
            vm(HEADS, ROWS, RES, dt=F32),
            vm(HALF * 8 + 8, ROWS, dt=F32),
            vm(HALF * 8 + 8, ROWS, dt=F32),
            vm(2, WIDTH, RES),
            vm(2, WIDTH, RES),
            vm(2, ROWS, WIDTH),
            vm(2, ROWS, WIDTH),
            vm(2, WIDTH, ROWS),
            vm(2, WIDTH, ROWS),
            vm(2, ROWS, WIDTH, dt=F32),
            vm(2, ROWS, WIDTH),
            vm(2, WIDTH, RES),
            vm(2, WIDTH, RES),
            vm(2, ROWS, WIDTH, dt=F32),
            vm(2, ROWS, WIDTH, dt=F32),
            vm(SEQS, ROWS, WIDTH, dt=F32),
            vm(SEQS, WIDTH, RES),
            vm(SEQS, PEERS, WIDTH, ROWS),
            vm(SEQS, ROWS, WIDTH),
            vm(SEQS, HALF, WIDTH),
            vm(HEADS, HALF, RES),
            vm(HEADS, HALF, RES),
            vm(HEADS, HALF, RES),
            vm(PEERS, HEADS, HALF, ROWS),
            dma((2,)), dma((2,)),
            dma((SEQS, PEERS)), dma((SEQS, PEERS)),
            dma((SEQS, PEERS)), dma((SEQS, PEERS)),
            dma((NCH, PEERS)), dma((NCH, PEERS)),
            dma((NCH,)), dma((NCH,)),
            dma((NCH,)), dma((NCH,)),
            dma((NCH, PEERS)), dma((NCH, PEERS)),
            dma((2,)), dma((2,)),
        ],
        compiler_params=pltpu.CompilerParams(
            collective_id=0, has_side_effects=True, vmem_limit_bytes=56 * 2**20
        ),
        name="attention_backward",
    )(x, pair, g, wq, wk, wv, wg, wo, wpt, mask, keep)


PB = 16


def pair_kernel(pair_ref, coef_ref, wpt_ref, out_ref):
    w = wpt_ref[...]
    w_hi, w_lo = split(w - jnp.mean(w, -1, keepdims=True))
    one = jnp.ones((1, 128), BF)

    def rows(n):
        return jnp.zeros((n, 128), BF)

    first = jnp.concatenate(
        [jnp.concatenate([w_hi, one, rows(7)], 0), jnp.concatenate([rows(9), one, rows(6)], 0)], 1
    )
    second = jnp.concatenate([jnp.concatenate([w_lo, rows(8)], 0), rows(16)], 1)
    right = jnp.concatenate([first, first, first, second], 0)
    for i in range(PB):
        cf = coef_ref[i * COEF : (i + 1) * COEF, :]
        hi = cf.astype(BF)
        rest = cf - hi.astype(F32)
        mid, low = split(rest)
        both = lax.dot_general(
            jnp.concatenate([hi, mid, low, hi], 0), right, (((0,), (0,)), ((), ())),
            preferred_element_type=F32,
        )
        out_ref[i] = both[:, :128] - pair_ref[i].astype(F32) * both[:, 128:]


def run_pair(pair, coef, wpt):
    n = pair.shape[0]
    return pl.pallas_call(
        pair_kernel,
        grid=(n // PB,),
        out_shape=jax.ShapeDtypeStruct(pair.shape, F32),
        in_specs=[
            pl.BlockSpec((PB, 128, 128), lambda i: (i, 0, 0)),
            pl.BlockSpec((PB * COEF, 128), lambda i: (i, 0)),
            pl.BlockSpec((HEADS, 128), lambda i: (0, 0)),
        ],
        out_specs=pl.BlockSpec((PB, 128, 128), lambda i: (i, 0, 0)),
        name="pair_gradient",
    )(pair, coef, wpt)


def body(x, pair, g, wq, wk, wv, wg, wo, wp, mask, keep):
    wpt = wp.T
    dx, coef = run_main(x, pair, g, wq, wk, wv, wg, wo, wpt, mask.reshape(8, 128), keep)
    return dx, run_pair(pair, coef, wpt)


def solution(mesh):
    return jax.shard_map(
        body,
        mesh=mesh,
        in_specs=(
            P("seq", "res", None),
            P("res", "seq", None),
            P("seq", "res", None),
            P(),
            P(),
            P(),
            P(),
            P(),
            P(),
            P(),
            P("seq"),
        ),
        out_specs=(P("seq", "res", None), P("res", "seq", None)),
        check_vma=False,
    )
```
